32 devices in a mesh: rows: 8 (over z, x), cls: 4 (over y, core).
Axes of the slice: x: 2, y: 2, z: 4, core: 2. Of those that a mesh axis runs over, the one named last changes fastest.
Arguments:
- centers: bfloat16 [2048, 1280], P('rows', 'cls'), may hold values from 0 to 4
- coefficients: float32 [1000, 2048], P('cls', 'rows'), may hold values from -0.6 to 0.6
- batch_features: bfloat16 [1024, 1280], P('rows', 'cls'), may hold values from 0 to 4
- batch_labels: int32 [1024], replicated, may hold values from 0 to 999
- batch_index: int32 [1024], replicated, may hold values from 0 to 2047
- subset_index: int32 [512], P('rows'), may hold values from 0 to 2047, as said below
- eigen_vectors: float32 [512, 512], P('rows'), may hold values from -0.25 to 0.25
- eigen_scale: float32 [512], replicated, may hold values from 0.2 to 2
Outputs:
- predicted: float32 [1000, 1024], P('cls')
- new_coefficients: float32 [1000, 2048], P('cls', 'rows')
The draws below stay inside these ranges and needn't reach their ends.
Inputs may be any that keep to these rules, and one draw needn't show every extreme that they name: `subset_index`: entry s lies among the centers (s // 64) * 256 to (s // 64 + 1) * 256 - 1; entry 0 is 0 and the last is 2047.
All inputs are finite; a program needn't handle non-finite values.
Results may differ from the reference program's by a relative error of at most 0.0003.
Values may be sent and summed in bfloat16 or wider, within the bound.
A program may use at most 64 MiB of HBM per device.

```python
import math
import jax
import jax.numpy as jnp
from jax import lax

D = 1280
C = 1000
Q = 512
B = 1024
CEN_DEV = 256
S_DEV = 64
M = 2048
S = 512
N_ROWS = 8


cluster_count = 16


def column_scales(key):
    return jnp.exp(jax.random.uniform(jax.random.fold_in(key, 11), (D,), jnp.float32, jnp.log(0.05), jnp.log(0.5)))


def cluster_means(key):
    return 1.2 * jax.random.normal(jax.random.fold_in(key, 13), (cluster_count, D), jnp.float32)


def scaled_features(key, count, salt):
    noise_key = jax.random.fold_in(key, salt)
    scale_key = jax.random.fold_in(key, salt + 1)
    member_key = jax.random.fold_in(key, salt + 2)
    members = jax.random.randint(member_key, (count,), 0, cluster_count, dtype=jnp.int32)
    centre = cluster_means(key)[members]
    noise_part = 0.6 * jnp.clip(jax.random.normal(noise_key, (count, D), jnp.float32), -4.0, 4.0)
    row_scale = jnp.exp(jax.random.uniform(scale_key, (count,), jnp.float32, jnp.log(0.5), jnp.log(2.0)))
    base = centre + noise_part
    scaled = jnp.maximum(base, 0.0) * row_scale[:, None] * column_scales(key)[None, :]
    return jnp.minimum(scaled, 4.0)


def draw_centers(key, part):
    return scaled_features(key, M, 21).astype(jnp.bfloat16)


def draw_batch_features(key, part):
    return scaled_features(key, B, 31).astype(jnp.bfloat16)


def draw_subset_index(key, part):
    positions = jnp.arange(S, dtype=jnp.int32)
    offsets = jax.random.randint(jax.random.fold_in(key, 41), (S,), 0, CEN_DEV, dtype=jnp.int32)
    chosen = positions // S_DEV * CEN_DEV + offsets
    chosen = chosen.at[0].set(0)
    return chosen.at[S - 1].set(M - 1)


def touch_ends(array, rng, least, high):
    longest = array.shape.index(max(array.shape))
    spots = []
    for shift in (0, 1):
        where = [jax.random.randint(jax.random.fold_in(rng, axis), (), 0, length) for axis, length in enumerate(array.shape)]
        where[longest] = (where[longest] + shift) % array.shape[longest]
        spots.append(tuple(where))
    return array.at[spots[0]].set(least).at[spots[1]].set(high)


def block_scale(stream_key, dims, cuts, least, largest):
    gain, own = 1.0, jax.random.fold_in(stream_key, 6)
    for dim, shards_of in cuts:
        steps = jnp.exp(jax.random.uniform(jax.random.fold_in(own, dim), (shards_of,), jnp.float32, least / len(cuts), largest / len(cuts)))
        gain = gain * jnp.repeat(steps, dims[dim] // shards_of).reshape([-1 if axis == dim else 1 for axis in range(len(dims))])
    return gain


def gaussian(key, shape, width, reach, cuts=(), kind=jnp.bfloat16):
    array = jax.random.normal(key, shape, jnp.float32) * width
    if len(cuts) > 0:
        array = block_scale(key, shape, cuts, -0.22, 0.18) * array
    return jnp.clip(array, min=-reach, max=reach).astype(kind)


def setup_inputs(seed: int = 0) -> dict:
    key_list = jax.random.split(jax.random.key(seed), 9)
    return {
        "centers": draw_centers(jax.random.fold_in(key_list[8], 71), 0),
        "coefficients": gaussian(key_list[1], (C, M), 0.1, 0.6, ((0, 4), (1, 8)), jnp.float32),
        "batch_features": draw_batch_features(jax.random.fold_in(key_list[8], 71), 0),
        "batch_labels": touch_ends(jax.random.randint(key_list[3], (B,), 0, C), jax.random.fold_in(key_list[3], 1), 0, C - 1).astype(jnp.int32),
        "batch_index": touch_ends(jax.random.randint(key_list[4], (B,), 0, M), jax.random.fold_in(key_list[4], 1), 0, M - 1).astype(jnp.int32),
        "subset_index": draw_subset_index(jax.random.fold_in(key_list[8], 71), 0),
        "eigen_vectors": gaussian(key_list[6], (S, Q), S ** -0.5, 0.25, ((0, 8),), jnp.float32),
        "eigen_scale": jnp.clip(jnp.exp(jax.random.uniform(key_list[7], (Q,), jnp.float32, math.log(0.2), math.log(2.0))), 0.2, 2.0),
    }


spread = 4.0
step_rate = 0.5

def kernel_block(inner, row_norm, col_norm):
    squared = row_norm[:, None] + col_norm[None, :] - 2.0 * inner
    return jnp.exp(-jnp.sqrt(jnp.maximum(squared, 0.0)) / spread)

def square_norm(features):
    return lax.optimization_barrier(jnp.sum(jnp.square(features.astype(jnp.float32)), axis=1))

def reference(centers, coefficients, batch_features, batch_labels, batch_index, subset_index, eigen_vectors, eigen_scale):
    batch_norm = square_norm(batch_features)
    center_blocks = centers.reshape(N_ROWS, CEN_DEV, D)
    coef_blocks = jnp.transpose(coefficients.reshape(C, N_ROWS, CEN_DEV), (1, 0, 2))

    def accumulate(totals, blocks_pair):
        center_rows, coef_rows = blocks_pair
        inner = jnp.dot(center_rows, batch_features.T, preferred_element_type=jnp.float32)
        kernel_rows = kernel_block(inner, square_norm(center_rows), batch_norm)
        return (totals + jnp.dot(coef_rows, kernel_rows, precision=lax.Precision.HIGHEST), None)
    predicted = lax.scan(accumulate, jnp.zeros((C, B), jnp.float32), (center_blocks, coef_blocks))[0]
    targets = (batch_labels[None, :] == jnp.arange(C, dtype=jnp.int32)[:, None]).astype(jnp.float32)
    gradient = predicted - targets
    subset_rows = centers[subset_index]
    subset_inner = jnp.dot(subset_rows, batch_features.T, preferred_element_type=jnp.float32)
    subset_kernel = kernel_block(subset_inner, square_norm(subset_rows), batch_norm)
    subset_err = jnp.dot(gradient, subset_kernel.T, precision=lax.Precision.HIGHEST)
    projected = jnp.dot(subset_err, eigen_vectors, precision=lax.Precision.HIGHEST)
    correction = jnp.dot(projected * eigen_scale[None, :], eigen_vectors.T, precision=lax.Precision.HIGHEST)
    updated = coefficients.at[:, batch_index].add(-step_rate * gradient)
    updated = updated.at[:, subset_index].add(step_rate * correction)
    return (predicted, updated)
```

```python
import functools

import jax
import jax.numpy as jnp
from jax import lax
from jax.experimental import pallas as pl
from jax.experimental.pallas import tpu as pltpu
from jax.sharding import PartitionSpec as P

spread = 4.0
step_rate = 0.5
HIGHEST = lax.Precision.HIGHEST
MESH = pl.DeviceIdType.MESH
NX = 2
NCORE = 2


def kernel_block(inner, row_norm, col_norm):
    squared = row_norm + col_norm - 2.0 * inner
    return jnp.exp(-jnp.sqrt(jnp.maximum(squared, 0.0)) / spread)


def square_norm(features):
    return jnp.sum(jnp.square(features.astype(jnp.float32)), axis=1)


def dot_nt(a, b, precision=None):
    return lax.dot_general(
        a, b, (((1,), (1,)), ((), ())),
        preferred_element_type=jnp.float32, precision=precision,
    )


def dot_tn(a, b, precision=None):
    return lax.dot_general(
        a, b, (((0,), (0,)), ((), ())),
        preferred_element_type=jnp.float32, precision=precision,
    )


def dot_nn(a, b, precision=None):
    return jnp.dot(a, b, preferred_element_type=jnp.float32, precision=precision)


def fused_kernel(
    rows, cls, class_count,
    cen_ref, coef_ref, bat_ref, lab_ref, idx_ref, sub_ref, eig_ref, scale_ref,
    pred_ref, new_ref,
    batch, cen, eig, coefp, sk, xsend, acc, xrecv, zrecv, pred, eall, gmat, upd,
    send_sem, recv_sem, xs_send, xs_recv,
):
    nz = rows // NX
    r = lax.axis_index("rows")
    c = lax.axis_index("cls")
    z, x = r // NX, r % NX
    y, k = c // NCORE, c % NCORE
    rx = z * NX + (1 - x)
    cy = (1 - y) * NCORE + k
    ck = y * NCORE + (1 - k)
    cyk = (1 - y) * NCORE + (1 - k)
    row_count = cen_ref.shape[0]
    cols = bat_ref.shape[0]
    subset_count = eig_ref.shape[0]
    eig_part = subset_count // cls
    first_row = r * row_count

    def zrow(d):
        return lax.rem(z + d, nz) * NX + x

    def zback(d):
        return lax.rem(z + nz - d, nz) * NX + x

    x_dev = (rx, c)
    y_dev = (r, cy)
    k_dev = (r, ck)

    def z_dev(d):
        return (zrow(d), c)

    barrier = pltpu.get_barrier_semaphore()
    partners = [x_dev, y_dev, k_dev] + [z_dev(d) for d in range(1, nz)]
    for dev in partners:
        pl.semaphore_signal(barrier, inc=1, device_id=dev, device_id_type=MESH)
    pl.semaphore_wait(barrier, len(partners))

    sent = []
    count = [0]

    def send(src, dst, dev):
        n = count[0]
        count[0] += 1
        copy = pltpu.make_async_remote_copy(
            src_ref=src, dst_ref=dst, send_sem=send_sem.at[n], recv_sem=recv_sem.at[n],
            device_id=dev, device_id_type=MESH,
        )
        copy.start()
        sent.append(copy)

        def arrive(slot):
            pltpu.make_async_remote_copy(
                src_ref=slot, dst_ref=slot, send_sem=send_sem.at[n], recv_sem=recv_sem.at[n],
                device_id=dev, device_id_type=MESH,
            ).wait_recv()

        return arrive

    core_waits = []
    pairs = [(r, c)]

    def to_core(src, row, col, other):
        core_waits.append((send(src, batch.at[row, col], k_dev), row, other))

    own = bat_ref
    z_waits = [send(own, batch.at[r, c], z_dev(d)) for d in range(1, nz)]
    y_waits = [(send(own, batch.at[r, c], y_dev), r)]
    x_waits = [(send(own, batch.at[r, c], x_dev), rx, c)]
    cen_k = send(cen_ref, cen.at[c], k_dev)
    cen_y = send(cen_ref, cen.at[c], y_dev)
    to_core(own, r, c, ck)
    eig_own = eig_ref.at[pl.ds(pl.multiple_of(c * eig_part, eig_part), eig_part)]
    batch[r, c] = bat_ref[...]
    cen[c] = cen_ref[...]
    eig[r, c] = eig_ref[pl.ds(pl.multiple_of(c * eig_part, eig_part), eig_part), :]
    coefp[...] = jnp.zeros_like(coefp)
    coefp[pl.ds(0, class_count), :] = coef_ref[...]
    for d in range(1, nz):
        row = zback(d)
        z_waits[d - 1](batch.at[row, c])
        y_waits.append((send(batch.at[row, c], batch.at[row, c], y_dev), row))
        x_waits.append((send(batch.at[row, c], batch.at[row, c], x_dev), row + 1 - 2 * x, c))
        to_core(batch.at[row, c], row, c, ck)
    cen_y(cen.at[cy])
    cen_yk = send(cen.at[cy], cen.at[cy], k_dev)
    for arrive, row in y_waits:
        arrive(batch.at[row, cy])
        x_waits.append((send(batch.at[row, cy], batch.at[row, cy], x_dev), row + 1 - 2 * x, cy))
        to_core(batch.at[row, cy], row, cy, cyk)
    ez_waits = [send(eig_own, eig.at[r, c], z_dev(d)) for d in range(1, nz)]
    for arrive, row, col in x_waits:
        arrive(batch.at[row, col])
        send_to = cyk if col is cy else ck
        to_core(batch.at[row, col], row, col, send_to)
    cen_k(cen.at[ck])
    cen_yk(cen.at[cyk])
    for arrive, row, col in core_waits:
        arrive(batch.at[row, col])

    ex_waits = [(send(eig_own, eig.at[r, c], x_dev), rx)]
    for d in range(1, nz):
        row = zback(d)
        ez_waits[d - 1](eig.at[row, c])
        ex_waits.append((send(eig.at[row, c], eig.at[row, c], x_dev), row + 1 - 2 * x))

    cen_norm = jnp.zeros((row_count, 1), jnp.float32)
    for q in range(cls):
        part = cen[q].astype(jnp.float32)
        cen_norm += jnp.sum(part * part, axis=1, keepdims=True)
    subset_local = sub_ref[...] - first_row
    pick = (
        lax.broadcasted_iota(jnp.int32, (row_count, subset_count), 0) == subset_local
    ).astype(jnp.float32)
    ones = jnp.ones((16, bat_ref.shape[1]), jnp.bfloat16)

    def part_pred(row):
        inner = jnp.zeros((row_count, cols), jnp.float32)
        norm = jnp.zeros((16, cols), jnp.float32)
        for q in range(cls):
            block = batch[row, q]
            inner += dot_nt(cen[q], block)
            wide = block.astype(jnp.float32)
            square = wide * wide
            high = square.astype(jnp.bfloat16)
            low = (square - high.astype(jnp.float32)).astype(jnp.bfloat16)
            norm += dot_nt(ones, high) + dot_nt(ones, low)
        kern = kernel_block(inner, cen_norm, norm[0:1, :])
        sk[row] = dot_tn(pick, kern, HIGHEST)
        return dot_nn(coefp[...], kern, HIGHEST)

    def x_copy(zz):
        return pltpu.make_async_remote_copy(
            src_ref=xsend.at[zz], dst_ref=xrecv.at[zz],
            send_sem=xs_send.at[zz], recv_sem=xs_recv.at[zz],
            device_id=x_dev, device_id_type=MESH,
        )

    def peer_chunk(zz, carry):
        xsend[zz] = part_pred(zz * NX + (1 - x))
        x_copy(zz).start()
        return carry

    def own_chunk(zz, carry):
        acc[zz] = part_pred(zz * NX + x)
        return carry

    lax.fori_loop(0, nz, peer_chunk, 0)
    lax.fori_loop(0, nz, own_chunk, 0)

    rs_waits = []
    for d in range(1, nz):
        zz = lax.rem(z + d, nz)
        x_copy(zz).wait()
        acc[zz] += xrecv[zz]
        rs_waits.append(send(acc.at[zz], zrecv.at[d - 1], z_dev(d)))
    x_copy(z).wait()
    total = acc[z] + xrecv[z]

    ey_waits, ek_waits = [], []
    ey_waits.append((send(eig_own, eig.at[r, c], y_dev), r))
    ek_waits.append((send(eig_own, eig.at[r, c], k_dev), r, ck))
    for d in range(1, nz):
        row = zback(d)
        ey_waits.append((send(eig.at[row, c], eig.at[row, c], y_dev), row))
        ek_waits.append((send(eig.at[row, c], eig.at[row, c], k_dev), row, ck))
    for arrive, row in ex_waits:
        arrive(eig.at[row, c])
        ey_waits.append((send(eig.at[row, c], eig.at[row, c], y_dev), row))
        ek_waits.append((send(eig.at[row, c], eig.at[row, c], k_dev), row, ck))

    for d in range(1, nz):
        rs_waits[d - 1](zrecv.at[d - 1])
        total += zrecv[d - 1]
    pred[r] = total

    ag_waits = [send(pred.at[r], pred.at[r], z_dev(d)) for d in range(1, nz)]
    ax_waits = [(send(pred.at[r], pred.at[r], x_dev), rx)]

    for arrive, row in ey_waits:
        arrive(eig.at[row, cy])
        ek_waits.append((send(eig.at[row, cy], eig.at[row, cy], k_dev), row, cyk))

    class_ids = lax.broadcasted_iota(jnp.int32, (coefp.shape[0], cols), 0) + c * class_count
    center_ids = lax.broadcasted_iota(jnp.int32, (row_count, cols), 0) + first_row

    def use_chunk(row, et):
        value = pred[row]
        pred_ref[:, pl.ds(pl.multiple_of(row * cols, cols), cols)] = value[0:class_count]
        grad = value - (lab_ref[pl.ds(row, 1), :] == class_ids).astype(jnp.float32)
        hit = (idx_ref[pl.ds(row, 1), :] == center_ids).astype(jnp.float32)
        upd[...] += dot_nt(grad, hit, HIGHEST)
        return et + dot_nt(sk[row], grad, HIGHEST)

    upd[...] = jnp.zeros_like(upd)
    et = use_chunk(r, jnp.zeros((subset_count, coefp.shape[0]), jnp.float32))
    for d in range(1, nz):
        row = zback(d)
        ag_waits[d - 1](pred.at[row])
        ax_waits.append((send(pred.at[row], pred.at[row], x_dev), row + 1 - 2 * x))
        et = use_chunk(row, et)
    for arrive, row, col in ek_waits:
        arrive(eig.at[row, col])
    whole = eig[...].reshape(rows * subset_count, eig_ref.shape[1])
    gmat[...] = dot_nt(eig_ref[...] * scale_ref[...], whole, HIGHEST)
    for arrive, row in ax_waits:
        arrive(pred.at[row])
        et = use_chunk(row, et)

    eall[r] = et
    fz_waits = [send(eall.at[r], eall.at[r], z_dev(d)) for d in range(1, nz)]
    fx_waits = [(send(eall.at[r], eall.at[r], x_dev), rx)]
    for d in range(1, nz):
        row = zback(d)
        fz_waits[d - 1](eall.at[row])
        fx_waits.append((send(eall.at[row], eall.at[row], x_dev), row + 1 - 2 * x))
    for arrive, row in fx_waits:
        arrive(eall.at[row])
    errors = eall[...].reshape(rows * subset_count, coefp.shape[0])
    correction = dot_nn(gmat[...], errors, HIGHEST)
    moved = dot_tn(correction, jnp.transpose(pick), HIGHEST)
    result = coefp[...] - step_rate * upd[...] + step_rate * moved
    new_ref[...] = result[0:class_count]
    for copy in sent:
        copy.wait_send()


def fused_shards(
    rows, cls,
    centers, coefficients, batch_features, batch_labels, batch_index,
    subset_index, eigen_vectors, eigen_scale,
):
    row_count, width = centers.shape
    class_count = coefficients.shape[0]
    cols = batch_features.shape[0]
    subset_count, eig_count = eigen_vectors.shape
    padded = -(-class_count // 8) * 8
    nz = rows // NX
    copies = 200
    f32 = jnp.float32
    vmem = pl.BlockSpec(memory_space=pltpu.VMEM)
    return pl.pallas_call(
        functools.partial(fused_kernel, rows, cls, class_count),
        out_shape=(
            jax.ShapeDtypeStruct((class_count, rows * cols), f32),
            jax.ShapeDtypeStruct((class_count, row_count), f32),
        ),
        in_specs=[vmem] * 8,
        out_specs=(vmem, vmem),
        scratch_shapes=[
            pltpu.VMEM((rows, cls, cols, width), jnp.bfloat16),
            pltpu.VMEM((cls, row_count, width), jnp.bfloat16),
            pltpu.VMEM((rows, cls, subset_count // cls, eig_count), f32),
            pltpu.VMEM((padded, row_count), f32),
            pltpu.VMEM((rows, subset_count, cols), f32),
            pltpu.VMEM((nz, padded, cols), f32),
            pltpu.VMEM((nz, padded, cols), f32),
            pltpu.VMEM((nz, padded, cols), f32),
            pltpu.VMEM((nz - 1, padded, cols), f32),
            pltpu.VMEM((rows, padded, cols), f32),
            pltpu.VMEM((rows, subset_count, padded), f32),
            pltpu.VMEM((subset_count, rows * subset_count), f32),
            pltpu.VMEM((padded, row_count), f32),
            pltpu.SemaphoreType.DMA((copies,)),
            pltpu.SemaphoreType.DMA((copies,)),
            pltpu.SemaphoreType.DMA((nz,)),
            pltpu.SemaphoreType.DMA((nz,)),
        ],
        compiler_params=pltpu.CompilerParams(
            collective_id=0, has_side_effects=True, vmem_limit_bytes=48 * 1024 * 1024
        ),
    )(
        centers, coefficients, batch_features,
        batch_labels.reshape(rows, cols), batch_index.reshape(rows, cols),
        subset_index.reshape(1, subset_count), eigen_vectors,
        eigen_scale.reshape(1, eig_count),
    )


def plain_shards(
    centers, coefficients, batch_features, batch_labels, batch_index,
    subset_index, eigen_vectors, eigen_scale,
):
    row_count = centers.shape[0]
    first_row = lax.axis_index("rows") * row_count
    subset_local = subset_index - first_row
    batch_rows = lax.all_gather(batch_features, "rows", axis=0, tiled=True)
    batch_whole = lax.all_gather(batch_rows, "cls", axis=1, tiled=True)
    batch_norm = square_norm(batch_whole)
    center_whole = lax.all_gather(centers, "cls", axis=1, tiled=True)
    inner = jnp.einsum("cd,bd->cb", center_whole, batch_whole, preferred_element_type=jnp.float32)
    kernel_centers = kernel_block(
        inner, square_norm(center_whole)[:, None], batch_norm[None, :]
    )
    subset_kernel = kernel_centers[subset_local]
    partial_pred = jnp.dot(coefficients, kernel_centers, precision=HIGHEST)
    class_count = coefficients.shape[0]
    class_start = lax.axis_index("cls") * class_count
    class_ids = jnp.arange(class_count, dtype=jnp.int32) + class_start
    targets = (batch_labels[None, :] == class_ids[:, None]).astype(jnp.float32)
    basis_part = jnp.dot(eigen_vectors.T, subset_kernel, precision=HIGHEST)
    predicted, basis_sum = lax.psum((partial_pred, basis_part), "rows")
    gradient = predicted - targets
    projected = jnp.dot(gradient, basis_sum.T, precision=HIGHEST)
    correction = jnp.dot(
        projected * eigen_scale[None, :], eigen_vectors.T, precision=HIGHEST
    )
    batch_local = batch_index - first_row
    is_owned = (batch_local >= 0) & (batch_local < row_count)
    batch_slot = jnp.where(is_owned, batch_local, row_count)
    updated = coefficients.at[:, batch_slot].add(-step_rate * gradient, mode="drop")
    updated = updated.at[:, subset_local].add(step_rate * correction)
    return (predicted, updated)


def solution(mesh):
    rows, cls = mesh.shape["rows"], mesh.shape["cls"]

    def shards(*args):
        cols = args[2].shape[0]
        fits = rows % NX == 0 and cls == 2 * NCORE and cols % 128 == 0
        if fits:
            return fused_shards(rows, cls, *args)
        return plain_shards(*args)

    return jax.shard_map(
        shards,
        mesh=mesh,
        in_specs=(
            P("rows", "cls"), P("cls", "rows"), P("rows", "cls"), P(), P(),
            P("rows"), P("rows", None), P(),
        ),
        out_specs=(P("cls", None), P("cls", "rows")),
        check_vma=False,
    )
```

```python
import functools

import jax
import jax.numpy as jnp
from jax import lax
from jax.experimental import pallas as pl
from jax.experimental.pallas import tpu as pltpu
from jax.sharding import PartitionSpec as P

spread = 4.0
step_rate = 0.5
HIGHEST = lax.Precision.HIGHEST
MESH = pl.DeviceIdType.MESH
NX = 2
NCORE = 2
LARGEST = 32767.0
STEPS = 256.0


def kernel_block(inner, row_norm, col_norm):
    squared = row_norm + col_norm - 2.0 * inner
    return jnp.exp(-jnp.sqrt(jnp.maximum(squared, 0.0)) / spread)


def square_norm(features):
    return jnp.sum(jnp.square(features.astype(jnp.float32)), axis=1)


def dot_nt(a, b):
    return lax.dot_general(
        a, b, (((1,), (1,)), ((), ())), preferred_element_type=jnp.float32
    )


def dot_nn(a, b):
    return jnp.dot(a, b, preferred_element_type=jnp.float32)


def split(value):
    high = value.astype(jnp.bfloat16)
    low = (value - high.astype(jnp.float32)).astype(jnp.bfloat16)
    return high, low


def pack(value, slot):
    count = value.shape[0]
    top = jnp.maximum(jnp.max(jnp.abs(value), axis=0, keepdims=True), 1e-37)
    code = jnp.clip(jnp.ceil(jnp.log2(top) * STEPS) + 1.0, -32000.0, 32000.0)
    gain = LARGEST * jnp.exp2(-code / STEPS)
    level = jnp.clip(jnp.round(value * gain), -LARGEST, LARGEST)
    slot[0:count, :] = level.astype(jnp.int32).astype(jnp.int16)
    codes = jnp.broadcast_to(code, (16, value.shape[1]))
    slot[count:count + 16, :] = codes.astype(jnp.int32).astype(jnp.int16)


def unpack(slot):
    count = slot.shape[0] - 16
    codes = slot[count:count + 16, :].astype(jnp.int32).astype(jnp.float32)
    unit = jnp.exp2(codes[0:1, :] / STEPS) / LARGEST
    return slot[0:count, :].astype(jnp.int32).astype(jnp.float32) * unit


def fused_kernel(
    rows, cls, class_count,
    cen_ref, coef_ref, bat_ref, lab_ref, idx_ref, sub_ref, eig_ref, scale_ref,
    pred_ref, new_ref,
    batch, cen, eig, sk, xsend, xrecv, acc, zsend, zrecv, pred, eall, upd,
    send_sem, recv_sem,
):
    nz = rows // NX
    r = lax.axis_index("rows")
    c = lax.axis_index("cls")
    z, x = r // NX, r % NX
    y, k = c // NCORE, c % NCORE
    flip = 1 - 2 * x
    cy = (1 - y) * NCORE + k
    ck = y * NCORE + (1 - k)
    cyk = (1 - y) * NCORE + (1 - k)
    width, row_count = cen_ref.shape
    cols = bat_ref.shape[1]
    subset_count = eig_ref.shape[0]
    eig_part = subset_count // cls
    padded = upd.shape[0]
    first_row = r * row_count
    x_dev, y_dev, k_dev = (r + flip, c), (r, cy), (r, ck)
    near = [lax.rem(z + nz - d, nz) * NX + x for d in range(nz)]
    far = [row + flip for row in near]
    ahead = [lax.rem(z + d, nz) for d in range(nz)]

    def z_dev(d):
        return (ahead[d] * NX + x, c)

    barrier = pltpu.get_barrier_semaphore()
    partners = [x_dev, y_dev, k_dev] + [z_dev(d) for d in range(1, nz)]
    for dev in partners:
        pl.semaphore_signal(barrier, inc=1, device_id=dev, device_id_type=MESH)

    def part(col):
        return pl.ds(pl.multiple_of(col * width, width), width)

    batch[r, part(c), :] = bat_ref[...]
    cen[part(c), :] = cen_ref[...]
    eig_rows = pl.ds(pl.multiple_of(c * eig_part, eig_part), eig_part)
    eig[r, c] = eig_ref[eig_rows, :]
    coef = coef_ref[...]
    if padded > class_count:
        upd[...] = jnp.zeros_like(upd)
        upd[0:class_count, :] = coef
        coef = upd[...]
    coef_high, coef_low = split(coef)
    subset_local = sub_ref[...] - first_row
    pick_t = jnp.transpose(
        (
            lax.broadcasted_iota(jnp.int32, (row_count, subset_count), 0) == subset_local
        ).astype(jnp.float32)
    ).astype(jnp.bfloat16)
    pl.semaphore_wait(barrier, len(partners))

    sent = []

    def send(src, dst, dev):
        n = len(sent)
        copy = pltpu.make_async_remote_copy(
            src_ref=src, dst_ref=dst, send_sem=send_sem.at[n], recv_sem=recv_sem.at[n],
            device_id=dev, device_id_type=MESH,
        )
        copy.start()
        sent.append(copy)

        def arrive(slot):
            pltpu.make_async_remote_copy(
                src_ref=slot, dst_ref=slot, send_sem=send_sem.at[n], recv_sem=recv_sem.at[n],
                device_id=dev, device_id_type=MESH,
            ).wait_recv()

        return arrive

    def slot(row, col):
        return batch.at[row, part(col)]

    def pass_on(row, col, dev):
        return send(slot(row, col), slot(row, col), dev)

    z_in = [None] + [pass_on(r, c, z_dev(d)) for d in range(1, nz)]
    y_in = [pass_on(r, c, y_dev)]
    x_in = [pass_on(r, c, x_dev)]
    cen_y = send(cen.at[part(c)], cen.at[part(c)], y_dev)
    cen_k = send(cen.at[part(c)], cen.at[part(c)], k_dev)
    near_in = [[pass_on(r, c, k_dev)]]
    for d in range(1, nz):
        z_in[d](slot(near[d], c))
        y_in.append(pass_on(near[d], c, y_dev))
        x_in.append(pass_on(near[d], c, x_dev))
        near_in.append([pass_on(near[d], c, k_dev)])
    cen_y(cen.at[part(cy)])
    cen_yk = send(cen.at[part(cy)], cen.at[part(cy)], k_dev)
    xy_in = []
    for d in range(nz):
        y_in[d](slot(near[d], cy))
        xy_in.append(pass_on(near[d], cy, x_dev))
        near_in[d].append(pass_on(near[d], cy, k_dev))
    own_eig = eig.at[r, c]
    ez_in = [None] + [send(own_eig, own_eig, z_dev(d)) for d in range(1, nz)]
    far_in = [[] for _ in range(nz)]

    cen_k(cen.at[part(ck)])
    cen_yk(cen.at[part(cyk)])
    cen_wide = jnp.transpose(cen[...].astype(jnp.float32))
    cen_norm = jnp.sum(cen_wide * cen_wide, axis=1, keepdims=True)
    cen_rows = cen_wide.astype(jnp.bfloat16)

    def part_pred(first, second):
        both = jnp.concatenate([batch[first], batch[second]], axis=1)
        wide = both.astype(jnp.float32)
        norm = jnp.sum(wide * wide, axis=0, keepdims=True)
        high, low = split(kernel_block(dot_nn(cen_rows, both), cen_norm, norm))
        sk_high = dot_nn(pick_t, high).astype(jnp.bfloat16)
        sk_low = dot_nn(pick_t, low).astype(jnp.bfloat16)
        for at, row in enumerate((first, second)):
            lanes = slice(at * cols, (at + 1) * cols)
            sk[row, 0:subset_count, :] = sk_high[:, lanes]
            sk[row, subset_count:2 * subset_count, :] = sk_low[:, lanes]
        return dot_nn(coef_high, high) + dot_nn(coef_high, low) + dot_nn(coef_low, high)

    sum_in = []
    for d in range(0, nz, 2):
        for i in (d, d + 1):
            x_in[i](slot(far[i], c))
            far_in[i].append(pass_on(far[i], c, k_dev))
        for i in (d, d + 1):
            near_in[i][0](slot(near[i], ck))
            near_in[i][1](slot(near[i], cyk))
        both = part_pred(near[d], near[d + 1])
        for at, i in enumerate((d, d + 1)):
            pack(both[:, at * cols:(at + 1) * cols], xsend.at[i])
    for i in range(nz):
        xy_in[i](slot(far[i], cy))
        far_in[i].append(pass_on(far[i], cy, k_dev))
    for i in range(nz):
        sum_in.append(send(xsend.at[i], xrecv.at[i], x_dev))
    ex_in = [send(own_eig, own_eig, x_dev)]
    for d in range(1, nz):
        ez_in[d](eig.at[near[d], c])
        ex_in.append(send(eig.at[near[d], c], eig.at[near[d], c], x_dev))
    for d in range(0, nz, 2):
        for i in (d, d + 1):
            far_in[i][0](slot(far[i], ck))
            far_in[i][1](slot(far[i], cyk))
        both = part_pred(far[d], far[d + 1])
        for at, i in enumerate((d, d + 1)):
            acc[i] = both[:, at * cols:(at + 1) * cols]

    rs_in = [None] * nz
    for d in range(1, nz):
        sum_in[d](xrecv.at[d])
        pack(acc[d] + unpack(xrecv.at[d]), zsend.at[d - 1])
        rs_in[d] = send(zsend.at[d - 1], zrecv.at[d - 1], z_dev(nz - d))
    sum_in[0](xrecv.at[0])
    total = acc[0] + unpack(xrecv.at[0])

    ey_in, ek_in = [], []

    def eig_on(row):
        ey_in.append((send(eig.at[row, c], eig.at[row, c], y_dev), row))
        ek_in.append((send(eig.at[row, c], eig.at[row, c], k_dev), row, ck))

    for row in near:
        eig_on(row)
    for arrive, row in zip(ex_in, far):
        arrive(eig.at[row, c])
        eig_on(row)

    for d in range(1, nz):
        rs_in[d](zrecv.at[d - 1])
        total += unpack(zrecv.at[d - 1])
    mine = far[0]
    pack(total, pred.at[mine])

    pz_in = [None] + [send(pred.at[mine], pred.at[mine], z_dev(d)) for d in range(1, nz)]
    px_in = [send(pred.at[mine], pred.at[mine], x_dev)]

    for arrive, row in ey_in:
        arrive(eig.at[row, cy])
        ek_in.append((send(eig.at[row, cy], eig.at[row, cy], k_dev), row, cyk))

    class_ids = lax.broadcasted_iota(jnp.int32, (padded, cols), 0) + c * class_count
    center_ids = lax.broadcasted_iota(jnp.int32, (row_count, cols), 0) + first_row

    def use_pair(pair, error, update):
        grads, hits, kernels = [], [], []
        for row in pair:
            value = unpack(pred.at[row])
            pred_ref[:, pl.ds(pl.multiple_of(row * cols, cols), cols)] = value[0:class_count]
            grads.append(value - (lab_ref[pl.ds(row, 1), :] == class_ids).astype(jnp.float32))
            hits.append((idx_ref[pl.ds(row, 1), :] == center_ids).astype(jnp.float32))
            kernels.append(sk[row])
        high, low = split(jnp.concatenate(grads, axis=1))
        hit = jnp.concatenate(hits, axis=1).astype(jnp.bfloat16)
        kernel_pair = jnp.concatenate(kernels, axis=1)
        two = dot_nt(kernel_pair, high)
        error += two[0:subset_count] + two[subset_count:]
        error += dot_nt(kernel_pair[0:subset_count], low)
        return error, update + dot_nt(high, hit) + dot_nt(low, hit)

    error = jnp.zeros((subset_count, padded), jnp.float32)
    update = jnp.zeros((padded, row_count), jnp.float32)
    for d in range(0, nz, 2):
        for i in (d, d + 1):
            if i > 0:
                pz_in[i](pred.at[far[i]])
                px_in.append(send(pred.at[far[i]], pred.at[far[i]], x_dev))
        error, update = use_pair((far[d], far[d + 1]), error, update)
    for arrive, row, col in ek_in:
        arrive(eig.at[row, col])
    whole_high, whole_low = split(eig[...].reshape(rows * subset_count, eig_ref.shape[1]))
    own_high, own_low = split(eig_ref[...] * scale_ref[...])
    metric = dot_nt(own_high, whole_high) + dot_nt(own_high, whole_low)
    metric_high, metric_low = split(metric + dot_nt(own_low, whole_high))
    for d in range(0, nz, 2):
        for i in (d, d + 1):
            px_in[i](pred.at[near[i]])
        error, update = use_pair((near[d], near[d + 1]), error, update)

    eall[r] = error
    fz_in = [None] + [send(eall.at[r], eall.at[r], z_dev(d)) for d in range(1, nz)]
    fx_in = [send(eall.at[r], eall.at[r], x_dev)]
    upd[...] = coef - step_rate * update
    for d in range(1, nz):
        fz_in[d](eall.at[near[d]])
        fx_in.append(send(eall.at[near[d]], eall.at[near[d]], x_dev))
    for d in range(nz):
        fx_in[d](eall.at[far[d]])
    high, low = split(eall[...].reshape(rows * subset_count, padded))
    correction = dot_nn(metric_high, high) + dot_nn(metric_high, low) + dot_nn(metric_low, high)
    high, low = split(jnp.transpose(correction))
    moved = dot_nn(high, pick_t) + dot_nn(low, pick_t)
    new_ref[...] = (upd[...] + step_rate * moved)[0:class_count]
    for copy in sent:
        copy.wait_send()


def fused_shards(
    rows, cls,
    centers, coefficients, batch_features, batch_labels, batch_index,
    subset_index, eigen_vectors, eigen_scale,
):
    row_count, width = centers.shape
    class_count = coefficients.shape[0]
    cols = batch_features.shape[0]
    subset_count, eig_count = eigen_vectors.shape
    padded = -(-class_count // 16) * 16
    nz = rows // NX
    copies = 13 * rows + 40
    f32, short = jnp.float32, jnp.int16
    vmem = pl.BlockSpec(memory_space=pltpu.VMEM)
    return pl.pallas_call(
        functools.partial(fused_kernel, rows, cls, class_count),
        out_shape=(
            jax.ShapeDtypeStruct((class_count, rows * cols), f32),
            jax.ShapeDtypeStruct((class_count, row_count), f32),
        ),
        in_specs=[vmem] * 8,
        out_specs=(vmem, vmem),
        scratch_shapes=[
            pltpu.VMEM((rows, cls * width, cols), jnp.bfloat16),
            pltpu.VMEM((cls * width, row_count), jnp.bfloat16),
            pltpu.VMEM((rows, cls, subset_count // cls, eig_count), f32),
            pltpu.VMEM((rows, 2 * subset_count, cols), jnp.bfloat16),
            pltpu.VMEM((nz, padded + 16, cols), short),
            pltpu.VMEM((nz, padded + 16, cols), short),
            pltpu.VMEM((nz, padded, cols), f32),
            pltpu.VMEM((nz - 1, padded + 16, cols), short),
            pltpu.VMEM((nz - 1, padded + 16, cols), short),
            pltpu.VMEM((rows, padded + 16, cols), short),
            pltpu.VMEM((rows, subset_count, padded), f32),
            pltpu.VMEM((padded, row_count), f32),
            pltpu.SemaphoreType.DMA((copies,)),
            pltpu.SemaphoreType.DMA((copies,)),
        ],
        compiler_params=pltpu.CompilerParams(
            collective_id=0, has_side_effects=True, vmem_limit_bytes=48 * 1024 * 1024
        ),
    )(
        centers.T, coefficients, batch_features.T,
        batch_labels.reshape(rows, cols), batch_index.reshape(rows, cols),
        subset_index.reshape(1, subset_count), eigen_vectors,
        eigen_scale.reshape(1, eig_count),
    )


def plain_shards(
    centers, coefficients, batch_features, batch_labels, batch_index,
    subset_index, eigen_vectors, eigen_scale,
):
    row_count = centers.shape[0]
    first_row = lax.axis_index("rows") * row_count
    subset_local = subset_index - first_row
    batch_rows = lax.all_gather(batch_features, "rows", axis=0, tiled=True)
    batch_whole = lax.all_gather(batch_rows, "cls", axis=1, tiled=True)
    batch_norm = square_norm(batch_whole)
    center_whole = lax.all_gather(centers, "cls", axis=1, tiled=True)
    inner = jnp.einsum("cd,bd->cb", center_whole, batch_whole, preferred_element_type=jnp.float32)
    kernel_centers = kernel_block(
        inner, square_norm(center_whole)[:, None], batch_norm[None, :]
    )
    subset_kernel = kernel_centers[subset_local]
    partial_pred = jnp.dot(coefficients, kernel_centers, precision=HIGHEST)
    class_count = coefficients.shape[0]
    class_start = lax.axis_index("cls") * class_count
    class_ids = jnp.arange(class_count, dtype=jnp.int32) + class_start
    targets = (batch_labels[None, :] == class_ids[:, None]).astype(jnp.float32)
    basis_part = jnp.dot(eigen_vectors.T, subset_kernel, precision=HIGHEST)
    predicted, basis_sum = lax.psum((partial_pred, basis_part), "rows")
    gradient = predicted - targets
    projected = jnp.dot(gradient, basis_sum.T, precision=HIGHEST)
    correction = jnp.dot(
        projected * eigen_scale[None, :], eigen_vectors.T, precision=HIGHEST
    )
    batch_local = batch_index - first_row
    is_owned = (batch_local >= 0) & (batch_local < row_count)
    batch_slot = jnp.where(is_owned, batch_local, row_count)
    updated = coefficients.at[:, batch_slot].add(-step_rate * gradient, mode="drop")
    updated = updated.at[:, subset_local].add(step_rate * correction)
    return (predicted, updated)


def solution(mesh):
    rows, cls = mesh.shape["rows"], mesh.shape["cls"]

    def shards(*args):
        cols = args[2].shape[0]
        fits = rows % (2 * NX) == 0 and cls == 2 * NCORE and cols % 128 == 0
        if fits:
            return fused_shards(rows, cls, *args)
        return plain_shards(*args)

    return jax.shard_map(
        shards,
        mesh=mesh,
        in_specs=(
            P("rows", "cls"), P("cls", "rows"), P("rows", "cls"), P(), P(),
            P("rows"), P("rows", None), P(),
        ),
        out_specs=(P("cls", None), P("cls", "rows")),
        check_vma=False,
    )
```

```python
import functools

import jax
import jax.numpy as jnp
from jax import lax
from jax.experimental import pallas as pl
from jax.experimental.pallas import tpu as pltpu
from jax.sharding import PartitionSpec as P

spread = 4.0
step_rate = 0.5
HIGHEST = lax.Precision.HIGHEST
MESH = pl.DeviceIdType.MESH
NX = 2
NCORE = 2
LARGEST = 32767.0
STEPS = 256.0


def kernel_block(inner, row_norm, col_norm):
    squared = row_norm + col_norm - 2.0 * inner
    return jnp.exp(-jnp.sqrt(jnp.maximum(squared, 0.0)) / spread)


def square_norm(features):
    return jnp.sum(jnp.square(features.astype(jnp.float32)), axis=1)


def dot_nt(a, b):
    return lax.dot_general(
        a, b, (((1,), (1,)), ((), ())), preferred_element_type=jnp.float32
    )


def dot_nn(a, b):
    return jnp.dot(a, b, preferred_element_type=jnp.float32)


def split(value):
    high = value.astype(jnp.bfloat16)
    low = (value - high.astype(jnp.float32)).astype(jnp.bfloat16)
    return high, low


def pack(value, slot):
    count = value.shape[0]
    top = jnp.maximum(jnp.max(jnp.abs(value), axis=0, keepdims=True), 1e-37)
    code = jnp.clip(jnp.ceil(jnp.log2(top) * STEPS) + 1.0, -32000.0, 32000.0)
    gain = LARGEST * jnp.exp2(-code / STEPS)
    level = jnp.clip(jnp.round(value * gain), -LARGEST, LARGEST)
    slot[0:count, :] = level.astype(jnp.int32).astype(jnp.int16)
    codes = jnp.broadcast_to(code, (16, value.shape[1]))
    slot[count:count + 16, :] = codes.astype(jnp.int32).astype(jnp.int16)


def unpack(slot):
    count = slot.shape[0] - 16
    codes = slot[count:count + 16, :].astype(jnp.int32).astype(jnp.float32)
    unit = jnp.exp2(codes[0:1, :] / STEPS) / LARGEST
    return slot[0:count, :].astype(jnp.int32).astype(jnp.float32) * unit


def fused_kernel(
    rows, cls, class_count,
    cen_hbm, coef_hbm, bat_hbm, lab_hbm, idx_hbm, sub_hbm, eig_hbm, scale_hbm,
    pred_ref, new_ref,
    batch, cen, eig, sk, xsend, xrecv, acc, zsend, zrecv, pred, eall, upd,
    coef_ref, lab_ref, idx_ref, sub_ref, eig_ref, scale_ref,
    send_sem, recv_sem, local_sem,
):
    nz = rows // NX
    r = lax.axis_index("rows")
    c = lax.axis_index("cls")
    z, x = r // NX, r % NX
    y, k = c // NCORE, c % NCORE
    flip = 1 - 2 * x
    cy = (1 - y) * NCORE + k
    ck = y * NCORE + (1 - k)
    cyk = (1 - y) * NCORE + (1 - k)
    width, row_count = cen_hbm.shape
    cols = bat_hbm.shape[1]
    subset_count = eig_ref.shape[0]
    eig_part = subset_count // cls
    padded = upd.shape[0]
    first_row = r * row_count
    x_dev, y_dev, k_dev = (r + flip, c), (r, cy), (r, ck)
    near = [lax.rem(z + nz - d, nz) * NX + x for d in range(nz)]
    far = [row + flip for row in near]
    ahead = [lax.rem(z + d, nz) for d in range(nz)]

    def z_dev(d):
        return (ahead[d] * NX + x, c)

    barrier = pltpu.get_barrier_semaphore()
    partners = [x_dev, y_dev, k_dev] + [z_dev(d) for d in range(1, nz)]
    for dev in partners:
        pl.semaphore_signal(barrier, inc=1, device_id=dev, device_id_type=MESH)

    def part(col):
        return pl.ds(pl.multiple_of(col * width, width), width)

    eig_rows = pl.ds(pl.multiple_of(c * eig_part, eig_part), eig_part)
    own_eig = eig_hbm.at[eig_rows]
    local = [
        pltpu.make_async_copy(src, dst, local_sem.at[n])
        for n, (src, dst) in enumerate((
            (sub_hbm, sub_ref), (cen_hbm, cen.at[part(c)]), (bat_hbm, batch.at[r, part(c)]),
            (coef_hbm, coef_ref), (lab_hbm, lab_ref), (idx_hbm, idx_ref),
            (eig_hbm, eig_ref), (own_eig, eig.at[r, c]), (scale_hbm, scale_ref),
        ))
    ]
    for copy in local:
        copy.start()
    pl.semaphore_wait(barrier, len(partners))

    sent = []

    def send(src, dst, dev):
        n = len(sent)
        copy = pltpu.make_async_remote_copy(
            src_ref=src, dst_ref=dst, send_sem=send_sem.at[n], recv_sem=recv_sem.at[n],
            device_id=dev, device_id_type=MESH,
        )
        copy.start()
        sent.append(copy)

        def arrive(slot):
            pltpu.make_async_remote_copy(
                src_ref=slot, dst_ref=slot, send_sem=send_sem.at[n], recv_sem=recv_sem.at[n],
                device_id=dev, device_id_type=MESH,
            ).wait_recv()

        return arrive

    def slot(row, col):
        return batch.at[row, part(col)]

    def pass_on(row, col, dev):
        return send(slot(row, col), slot(row, col), dev)

    z_in = [None] + [send(bat_hbm, slot(r, c), z_dev(d)) for d in range(1, nz)]
    x_in = [send(bat_hbm, slot(r, c), x_dev)]
    y_in = [send(bat_hbm, slot(r, c), y_dev)]
    cen_y = send(cen_hbm, cen.at[part(c)], y_dev)
    near_in = [[send(bat_hbm, slot(r, c), k_dev)]]
    cen_k = send(cen_hbm, cen.at[part(c)], k_dev)

    for copy in local:
        copy.wait()
    coef = coef_ref[...]
    if padded > class_count:
        upd[...] = jnp.zeros_like(upd)
        upd[0:class_count, :] = coef
        coef = upd[...]
    coef_high, coef_low = split(coef)
    subset_local = sub_ref[...] - first_row
    pick_t = jnp.transpose(
        (
            lax.broadcasted_iota(jnp.int32, (row_count, subset_count), 0) == subset_local
        ).astype(jnp.float32)
    ).astype(jnp.bfloat16)
    for d in range(1, nz):
        z_in[d](slot(near[d], c))
        y_in.append(pass_on(near[d], c, y_dev))
        x_in.append(pass_on(near[d], c, x_dev))
        near_in.append([pass_on(near[d], c, k_dev)])
    cen_y(cen.at[part(cy)])
    cen_yk = send(cen.at[part(cy)], cen.at[part(cy)], k_dev)
    xy_in = []
    for d in range(nz):
        y_in[d](slot(near[d], cy))
        if d < nz - 1:
            xy_in.append(pass_on(near[d], cy, x_dev))
        near_in[d].append(pass_on(near[d], cy, k_dev))
    ez_in = [None] + [send(own_eig, eig.at[r, c], z_dev(d)) for d in range(1, nz)]
    far_in = [[] for _ in range(nz)]

    cen_k(cen.at[part(ck)])
    cen_yk(cen.at[part(cyk)])
    cen_wide = jnp.transpose(cen[...].astype(jnp.float32))
    cen_norm = jnp.sum(cen_wide * cen_wide, axis=1, keepdims=True)
    cen_rows = cen_wide.astype(jnp.bfloat16)

    def part_pred(first, second):
        both = jnp.concatenate([batch[first], batch[second]], axis=1)
        wide = both.astype(jnp.float32)
        norm = jnp.sum(wide * wide, axis=0, keepdims=True)
        high, low = split(kernel_block(dot_nn(cen_rows, both), cen_norm, norm))
        sk_high = dot_nn(pick_t, high).astype(jnp.bfloat16)
        sk_low = dot_nn(pick_t, low).astype(jnp.bfloat16)
        for at, row in enumerate((first, second)):
            lanes = slice(at * cols, (at + 1) * cols)
            sk[row, 0:subset_count, :] = sk_high[:, lanes]
            sk[row, subset_count:2 * subset_count, :] = sk_low[:, lanes]
        return dot_nn(coef_high, high) + dot_nn(coef_high, low) + dot_nn(coef_low, high)

    for i in range(nz - 1, -1, -1):
        x_in[i](slot(far[i], c))
        if i == nz - 1:
            xy_in.append(pass_on(far[i], c, y_dev))
        far_in[i].append(pass_on(far[i], c, k_dev))
    sum_in = []
    for d in range(0, nz, 2):
        for i in (d, d + 1):
            near_in[i][0](slot(near[i], ck))
            near_in[i][1](slot(near[i], cyk))
        both = part_pred(near[d], near[d + 1])
        for at, i in enumerate((d, d + 1)):
            pack(both[:, at * cols:(at + 1) * cols], xsend.at[i])
            sum_in.append(send(xsend.at[i], xrecv.at[i], x_dev))
        for i in (d, d + 1):
            xy_in[i](slot(far[i], cy))
            far_in[i].append(pass_on(far[i], cy, k_dev))
    ex_in = [send(own_eig, eig.at[r, c], x_dev)]
    for d in range(1, nz):
        ez_in[d](eig.at[near[d], c])
        ex_in.append(send(eig.at[near[d], c], eig.at[near[d], c], x_dev))
    for d in range(0, nz, 2):
        for i in (d, d + 1):
            far_in[i][0](slot(far[i], ck))
            far_in[i][1](slot(far[i], cyk))
        both = part_pred(far[d], far[d + 1])
        for at, i in enumerate((d, d + 1)):
            acc[i] = both[:, at * cols:(at + 1) * cols]

    rs_in = [None] * nz
    for d in range(1, nz):
        sum_in[d](xrecv.at[d])
        pack(acc[d] + unpack(xrecv.at[d]), zsend.at[d - 1])
        rs_in[d] = send(zsend.at[d - 1], zrecv.at[d - 1], z_dev(nz - d))
    sum_in[0](xrecv.at[0])
    total = acc[0] + unpack(xrecv.at[0])

    ey_in, ek_in = [], []

    def eig_on(row):
        ey_in.append((send(eig.at[row, c], eig.at[row, c], y_dev), row))
        ek_in.append((send(eig.at[row, c], eig.at[row, c], k_dev), row, ck))

    for row in near:
        eig_on(row)
    for arrive, row in zip(ex_in, far):
        arrive(eig.at[row, c])
        eig_on(row)

    for d in range(1, nz):
        rs_in[d](zrecv.at[d - 1])
        total += unpack(zrecv.at[d - 1])
    mine = far[0]
    pack(total, pred.at[mine])

    pz_in = [None] + [send(pred.at[mine], pred.at[mine], z_dev(d)) for d in range(1, nz)]
    px_in = [send(pred.at[mine], pred.at[mine], x_dev)]

    for arrive, row in ey_in:
        arrive(eig.at[row, cy])
        ek_in.append((send(eig.at[row, cy], eig.at[row, cy], k_dev), row, cyk))

    class_ids = lax.broadcasted_iota(jnp.int32, (padded, cols), 0) + c * class_count
    center_ids = lax.broadcasted_iota(jnp.int32, (row_count, cols), 0) + first_row

    def use_pair(pair, error, update):
        grads, hits, kernels = [], [], []
        for row in pair:
            value = unpack(pred.at[row])
            pred_ref[:, pl.ds(pl.multiple_of(row * cols, cols), cols)] = value[0:class_count]
            grads.append(value - (lab_ref[pl.ds(row, 1), :] == class_ids).astype(jnp.float32))
            hits.append((idx_ref[pl.ds(row, 1), :] == center_ids).astype(jnp.float32))
            kernels.append(sk[row])
        high, low = split(jnp.concatenate(grads, axis=1))
        hit = jnp.concatenate(hits, axis=1).astype(jnp.bfloat16)
        kernel_pair = jnp.concatenate(kernels, axis=1)
        two = dot_nt(kernel_pair, high)
        error += two[0:subset_count] + two[subset_count:]
        error += dot_nt(kernel_pair[0:subset_count], low)
        return error, update + dot_nt(high, hit) + dot_nt(low, hit)

    error = jnp.zeros((subset_count, padded), jnp.float32)
    update = jnp.zeros((padded, row_count), jnp.float32)
    for d in range(0, nz, 2):
        for i in (d, d + 1):
            if i > 0:
                pz_in[i](pred.at[far[i]])
                px_in.append(send(pred.at[far[i]], pred.at[far[i]], x_dev))
        error, update = use_pair((far[d], far[d + 1]), error, update)
    for arrive, row, col in ek_in:
        arrive(eig.at[row, col])
    whole_high, whole_low = split(eig[...].reshape(rows * subset_count, eig_ref.shape[1]))
    own_high, own_low = split(eig_ref[...] * scale_ref[...])
    metric = dot_nt(own_high, whole_high) + dot_nt(own_high, whole_low)
    metric_high, metric_low = split(metric + dot_nt(own_low, whole_high))
    for d in range(0, nz, 2):
        for i in (d, d + 1):
            px_in[i](pred.at[near[i]])
        error, update = use_pair((near[d], near[d + 1]), error, update)

    pack(error, eall.at[r])
    fz_in = [None] + [send(eall.at[r], eall.at[r], z_dev(d)) for d in range(1, nz)]
    fx_in = [send(eall.at[r], eall.at[r], x_dev)]
    upd[...] = coef - step_rate * update
    for d in range(1, nz):
        fz_in[d](eall.at[near[d]])
        fx_in.append(send(eall.at[near[d]], eall.at[near[d]], x_dev))
    for d in range(nz):
        fx_in[d](eall.at[far[d]])
    high, low = split(jnp.concatenate([unpack(eall.at[row]) for row in range(rows)], axis=0))
    correction = dot_nn(metric_high, high) + dot_nn(metric_high, low) + dot_nn(metric_low, high)
    high, low = split(jnp.transpose(correction))
    moved = dot_nn(high, pick_t) + dot_nn(low, pick_t)
    new_ref[...] = (upd[...] + step_rate * moved)[0:class_count]
    for copy in sent:
        copy.wait_send()


def fused_shards(
    rows, cls,
    centers, coefficients, batch_features, batch_labels, batch_index,
    subset_index, eigen_vectors, eigen_scale,
):
    row_count, width = centers.shape
    class_count = coefficients.shape[0]
    cols = batch_features.shape[0]
    subset_count, eig_count = eigen_vectors.shape
    padded = -(-class_count // 16) * 16
    nz = rows // NX
    copies = 13 * rows + 40
    f32, short = jnp.float32, jnp.int16
    vmem = pl.BlockSpec(memory_space=pltpu.VMEM)
    return pl.pallas_call(
        functools.partial(fused_kernel, rows, cls, class_count),
        out_shape=(
            jax.ShapeDtypeStruct((class_count, rows * cols), f32),
            jax.ShapeDtypeStruct((class_count, row_count), f32),
        ),
        in_specs=[pl.BlockSpec(memory_space=pltpu.HBM)] * 8,
        out_specs=(vmem, vmem),
        scratch_shapes=[
            pltpu.VMEM((rows, cls * width, cols), jnp.bfloat16),
            pltpu.VMEM((cls * width, row_count), jnp.bfloat16),
            pltpu.VMEM((rows, cls, subset_count // cls, eig_count), f32),
            pltpu.VMEM((rows, 2 * subset_count, cols), jnp.bfloat16),
            pltpu.VMEM((nz, padded + 16, cols), short),
            pltpu.VMEM((nz, padded + 16, cols), short),
            pltpu.VMEM((nz, padded, cols), f32),
            pltpu.VMEM((nz - 1, padded + 16, cols), short),
            pltpu.VMEM((nz - 1, padded + 16, cols), short),
            pltpu.VMEM((rows, padded + 16, cols), short),
            pltpu.VMEM((rows, subset_count + 16, padded), short),
            pltpu.VMEM((padded, row_count), f32),
            pltpu.VMEM((class_count, row_count), f32),
            pltpu.VMEM((rows, cols), jnp.int32),
            pltpu.VMEM((rows, cols), jnp.int32),
            pltpu.VMEM((1, subset_count), jnp.int32),
            pltpu.VMEM((subset_count, eig_count), f32),
            pltpu.VMEM((1, eig_count), f32),
            pltpu.SemaphoreType.DMA((copies,)),
            pltpu.SemaphoreType.DMA((copies,)),
            pltpu.SemaphoreType.DMA((9,)),
        ],
        compiler_params=pltpu.CompilerParams(
            collective_id=0, has_side_effects=True, vmem_limit_bytes=48 * 1024 * 1024
        ),
    )(
        centers.T, coefficients, batch_features.T,
        batch_labels.reshape(rows, cols), batch_index.reshape(rows, cols),
        subset_index.reshape(1, subset_count), eigen_vectors,
        eigen_scale.reshape(1, eig_count),
    )


def plain_shards(
    centers, coefficients, batch_features, batch_labels, batch_index,
    subset_index, eigen_vectors, eigen_scale,
):
    row_count = centers.shape[0]
    first_row = lax.axis_index("rows") * row_count
    subset_local = subset_index - first_row
    batch_rows = lax.all_gather(batch_features, "rows", axis=0, tiled=True)
    batch_whole = lax.all_gather(batch_rows, "cls", axis=1, tiled=True)
    batch_norm = square_norm(batch_whole)
    center_whole = lax.all_gather(centers, "cls", axis=1, tiled=True)
    inner = jnp.einsum("cd,bd->cb", center_whole, batch_whole, preferred_element_type=jnp.float32)
    kernel_centers = kernel_block(
        inner, square_norm(center_whole)[:, None], batch_norm[None, :]
    )
    subset_kernel = kernel_centers[subset_local]
    partial_pred = jnp.dot(coefficients, kernel_centers, precision=HIGHEST)
    class_count = coefficients.shape[0]
    class_start = lax.axis_index("cls") * class_count
    class_ids = jnp.arange(class_count, dtype=jnp.int32) + class_start
    targets = (batch_labels[None, :] == class_ids[:, None]).astype(jnp.float32)
    basis_part = jnp.dot(eigen_vectors.T, subset_kernel, precision=HIGHEST)
    predicted, basis_sum = lax.psum((partial_pred, basis_part), "rows")
    gradient = predicted - targets
    projected = jnp.dot(gradient, basis_sum.T, precision=HIGHEST)
    correction = jnp.dot(
        projected * eigen_scale[None, :], eigen_vectors.T, precision=HIGHEST
    )
    batch_local = batch_index - first_row
    is_owned = (batch_local >= 0) & (batch_local < row_count)
    batch_slot = jnp.where(is_owned, batch_local, row_count)
    updated = coefficients.at[:, batch_slot].add(-step_rate * gradient, mode="drop")
    updated = updated.at[:, subset_local].add(step_rate * correction)
    return (predicted, updated)


def solution(mesh):
    rows, cls = mesh.shape["rows"], mesh.shape["cls"]

    def shards(*args):
        cols = args[2].shape[0]
        fits = rows % (2 * NX) == 0 and cls == 2 * NCORE and cols % 128 == 0
        if fits:
            return fused_shards(rows, cls, *args)
        return plain_shards(*args)

    return jax.shard_map(
        shards,
        mesh=mesh,
        in_specs=(
            P("rows", "cls"), P("cls", "rows"), P("rows", "cls"), P(), P(),
            P("rows"), P("rows", None), P(),
        ),
        out_specs=(P("cls", None), P("cls", "rows")),
        check_vma=False,
    )
```

```python
import functools

import jax
import jax.numpy as jnp
from jax import lax
from jax.experimental import pallas as pl
from jax.experimental.pallas import tpu as pltpu
from jax.sharding import PartitionSpec as P

spread = 4.0
step_rate = 0.5
HIGHEST = lax.Precision.HIGHEST
MESH = pl.DeviceIdType.MESH
NX = 2
NCORE = 2
LARGEST = 32767.0
STEPS = 256.0


def kernel_block(inner, row_norm, col_norm):
    squared = row_norm + col_norm - 2.0 * inner
    return jnp.exp(-jnp.sqrt(jnp.maximum(squared, 0.0)) / spread)


def square_norm(features):
    return jnp.sum(jnp.square(features.astype(jnp.float32)), axis=1)


def dot_nt(a, b):
    return lax.dot_general(
        a, b, (((1,), (1,)), ((), ())), preferred_element_type=jnp.float32
    )


def dot_nn(a, b):
    return jnp.dot(a, b, preferred_element_type=jnp.float32)


def split(value):
    high = value.astype(jnp.bfloat16)
    low = (value - high.astype(jnp.float32)).astype(jnp.bfloat16)
    return high, low


def pack(value, slot):
    count = value.shape[0]
    top = jnp.maximum(jnp.max(jnp.abs(value), axis=0, keepdims=True), 1e-37)
    code = jnp.clip(jnp.ceil(jnp.log2(top) * STEPS) + 1.0, -32000.0, 32000.0)
    gain = LARGEST * jnp.exp2(-code / STEPS)
    level = jnp.clip(jnp.round(value * gain), -LARGEST, LARGEST)
    slot[0:count, :] = level.astype(jnp.int32).astype(jnp.int16)
    codes = jnp.broadcast_to(code, (16, value.shape[1]))
    slot[count:count + 16, :] = codes.astype(jnp.int32).astype(jnp.int16)


def unpack(slot):
    count = slot.shape[0] - 16
    codes = slot[count:count + 16, :].astype(jnp.int32).astype(jnp.float32)
    unit = jnp.exp2(codes[0:1, :] / STEPS) / LARGEST
    return slot[0:count, :].astype(jnp.int32).astype(jnp.float32) * unit


def fused_kernel(
    rows, cls, class_count,
    cen_hbm, coef_hbm, bat_hbm, lab_hbm, idx_hbm, sub_hbm, eig_hbm, scale_hbm,
    pred_hbm, new_hbm,
    batch, cen, eig, sk, xsend, xrecv, acc, zsend, zrecv, pred, eall, upd,
    pred_ref, coef_ref, lab_ref, idx_ref, sub_ref, eig_ref, scale_ref,
    send_sem, recv_sem, local_sem,
):
    nz = rows // NX
    r = lax.axis_index("rows")
    c = lax.axis_index("cls")
    z, x = r // NX, r % NX
    y, k = c // NCORE, c % NCORE
    flip = 1 - 2 * x
    cy = (1 - y) * NCORE + k
    ck = y * NCORE + (1 - k)
    cyk = (1 - y) * NCORE + (1 - k)
    width, row_count = cen_hbm.shape
    cols = bat_hbm.shape[1]
    subset_count = eig_ref.shape[0]
    eig_part = subset_count // cls
    padded = upd.shape[0]
    first_row = r * row_count
    x_dev, y_dev, k_dev = (r + flip, c), (r, cy), (r, ck)
    near = [lax.rem(z + nz - d, nz) * NX + x for d in range(nz)]
    far = [row + flip for row in near]
    ahead = [lax.rem(z + d, nz) for d in range(nz)]

    def z_dev(d):
        return (ahead[d] * NX + x, c)

    barrier = pltpu.get_barrier_semaphore()
    partners = [x_dev, y_dev, k_dev] + [z_dev(d) for d in range(1, nz)]
    for dev in partners:
        pl.semaphore_signal(barrier, inc=1, device_id=dev, device_id_type=MESH)

    def part(col):
        return pl.ds(pl.multiple_of(col * width, width), width)

    eig_rows = pl.ds(pl.multiple_of(c * eig_part, eig_part), eig_part)
    own_eig = eig_hbm.at[eig_rows]
    local = [
        pltpu.make_async_copy(src, dst, local_sem.at[n])
        for n, (src, dst) in enumerate((
            (sub_hbm, sub_ref), (cen_hbm, cen.at[part(c)]), (bat_hbm, batch.at[r, part(c)]),
            (coef_hbm, coef_ref), (lab_hbm, lab_ref), (idx_hbm, idx_ref),
            (eig_hbm, eig_ref), (own_eig, eig.at[r, c]), (scale_hbm, scale_ref),
        ))
    ]
    for copy in local:
        copy.start()
    pl.semaphore_wait(barrier, len(partners))

    sent = []

    def send(src, dst, dev):
        n = len(sent)
        copy = pltpu.make_async_remote_copy(
            src_ref=src, dst_ref=dst, send_sem=send_sem.at[n], recv_sem=recv_sem.at[n],
            device_id=dev, device_id_type=MESH,
        )
        copy.start()
        sent.append(copy)

        def arrive(slot):
            pltpu.make_async_remote_copy(
                src_ref=slot, dst_ref=slot, send_sem=send_sem.at[n], recv_sem=recv_sem.at[n],
                device_id=dev, device_id_type=MESH,
            ).wait_recv()

        return arrive

    def slot(row, col):
        return batch.at[row, part(col)]

    def pass_on(row, col, dev):
        return send(slot(row, col), slot(row, col), dev)

    z_in = [None] + [send(bat_hbm, slot(r, c), z_dev(d)) for d in range(1, nz)]
    x_in = [send(bat_hbm, slot(r, c), x_dev)]
    y_in = [send(bat_hbm, slot(r, c), y_dev)]
    cen_y = send(cen_hbm, cen.at[part(c)], y_dev)
    near_in = [[send(bat_hbm, slot(r, c), k_dev)]]
    cen_k = send(cen_hbm, cen.at[part(c)], k_dev)

    for copy in local:
        copy.wait()
    coef = coef_ref[...]
    if padded > class_count:
        upd[...] = jnp.zeros_like(upd)
        upd[0:class_count, :] = coef
        coef = upd[...]
    coef_high, coef_low = split(coef)
    subset_local = sub_ref[...] - first_row
    pick_t = jnp.transpose(
        (
            lax.broadcasted_iota(jnp.int32, (row_count, subset_count), 0) == subset_local
        ).astype(jnp.float32)
    ).astype(jnp.bfloat16)
    for d in range(1, nz):
        z_in[d](slot(near[d], c))
        y_in.append(pass_on(near[d], c, y_dev))
        x_in.append(pass_on(near[d], c, x_dev))
        near_in.append([pass_on(near[d], c, k_dev)])
    cen_y(cen.at[part(cy)])
    cen_yk = send(cen.at[part(cy)], cen.at[part(cy)], k_dev)
    xy_in = []
    for d in range(nz):
        y_in[d](slot(near[d], cy))
        if d < nz - 1:
            xy_in.append(pass_on(near[d], cy, x_dev))
        near_in[d].append(pass_on(near[d], cy, k_dev))
    ez_in = [None] + [send(own_eig, eig.at[r, c], z_dev(d)) for d in range(1, nz)]
    far_in = [[] for _ in range(nz)]

    cen_k(cen.at[part(ck)])
    cen_yk(cen.at[part(cyk)])
    cen_wide = jnp.transpose(cen[...].astype(jnp.float32))
    cen_norm = jnp.sum(cen_wide * cen_wide, axis=1, keepdims=True)
    cen_rows = cen_wide.astype(jnp.bfloat16)

    def part_pred(first, second):
        both = jnp.concatenate([batch[first], batch[second]], axis=1)
        wide = both.astype(jnp.float32)
        norm = jnp.sum(wide * wide, axis=0, keepdims=True)
        high, low = split(kernel_block(dot_nn(cen_rows, both), cen_norm, norm))
        sk_high = dot_nn(pick_t, high).astype(jnp.bfloat16)
        sk_low = dot_nn(pick_t, low).astype(jnp.bfloat16)
        for at, row in enumerate((first, second)):
            lanes = slice(at * cols, (at + 1) * cols)
            sk[row, 0:subset_count, :] = sk_high[:, lanes]
            sk[row, subset_count:2 * subset_count, :] = sk_low[:, lanes]
        return dot_nn(coef_high, high) + dot_nn(coef_high, low) + dot_nn(coef_low, high)

    for i in range(nz - 1, -1, -1):
        x_in[i](slot(far[i], c))
        if i == nz - 1:
            xy_in.append(pass_on(far[i], c, y_dev))
        far_in[i].append(pass_on(far[i], c, k_dev))
    sum_in = []
    for d in range(0, nz, 2):
        for i in (d, d + 1):
            near_in[i][0](slot(near[i], ck))
            near_in[i][1](slot(near[i], cyk))
        both = part_pred(near[d], near[d + 1])
        for at, i in enumerate((d, d + 1)):
            pack(both[:, at * cols:(at + 1) * cols], xsend.at[i])
            sum_in.append(send(xsend.at[i], xrecv.at[i], x_dev))
        for i in (d, d + 1):
            xy_in[i](slot(far[i], cy))
            far_in[i].append(pass_on(far[i], cy, k_dev))
    ex_in = [send(own_eig, eig.at[r, c], x_dev)]
    for d in range(1, nz):
        ez_in[d](eig.at[near[d], c])
        ex_in.append(send(eig.at[near[d], c], eig.at[near[d], c], x_dev))
    for d in range(0, nz, 2):
        for i in (d, d + 1):
            far_in[i][0](slot(far[i], ck))
            far_in[i][1](slot(far[i], cyk))
        both = part_pred(far[d], far[d + 1])
        for at, i in enumerate((d, d + 1)):
            acc[i] = both[:, at * cols:(at + 1) * cols]

    rs_in = [None] * nz
    for d in range(1, nz):
        sum_in[d](xrecv.at[d])
        pack(acc[d] + unpack(xrecv.at[d]), zsend.at[d - 1])
        rs_in[d] = send(zsend.at[d - 1], zrecv.at[d - 1], z_dev(nz - d))
    sum_in[0](xrecv.at[0])
    total = acc[0] + unpack(xrecv.at[0])

    ey_in, ek_in = [], []

    def eig_on(row):
        ey_in.append((send(eig.at[row, c], eig.at[row, c], y_dev), row))
        ek_in.append((send(eig.at[row, c], eig.at[row, c], k_dev), row, ck))

    for row in near:
        eig_on(row)
    for arrive, row in zip(ex_in, far):
        arrive(eig.at[row, c])
        eig_on(row)

    for d in range(1, nz):
        rs_in[d](zrecv.at[d - 1])
        total += unpack(zrecv.at[d - 1])
    mine = far[0]
    pack(total, pred.at[mine])

    pz_in = [None] + [send(pred.at[mine], pred.at[mine], z_dev(d)) for d in range(1, nz)]
    px_in = [send(pred.at[mine], pred.at[mine], x_dev)]

    for arrive, row in ey_in:
        arrive(eig.at[row, cy])
        ek_in.append((send(eig.at[row, cy], eig.at[row, cy], k_dev), row, cyk))

    class_ids = lax.broadcasted_iota(jnp.int32, (padded, cols), 0) + c * class_count
    center_ids = lax.broadcasted_iota(jnp.int32, (row_count, cols), 0) + first_row

    leaving = []

    def use_pair(pair, error, update):
        grads, hits, kernels = [], [], []
        for row in pair:
            value = unpack(pred.at[row])
            pred_ref[row] = value[0:class_count]
            columns = pl.ds(pl.multiple_of(row * cols, cols), cols)
            n = 9 + len(leaving)
            leaving.append(
                pltpu.make_async_copy(pred_ref.at[row], pred_hbm.at[:, columns], local_sem.at[n])
            )
            leaving[-1].start()
            grads.append(value - (lab_ref[pl.ds(row, 1), :] == class_ids).astype(jnp.float32))
            hits.append((idx_ref[pl.ds(row, 1), :] == center_ids).astype(jnp.float32))
            kernels.append(sk[row])
        high, low = split(jnp.concatenate(grads, axis=1))
        hit = jnp.concatenate(hits, axis=1).astype(jnp.bfloat16)
        kernel_pair = jnp.concatenate(kernels, axis=1)
        two = dot_nt(kernel_pair, high)
        error += two[0:subset_count] + two[subset_count:]
        error += dot_nt(kernel_pair[0:subset_count], low)
        return error, update + dot_nt(high, hit) + dot_nt(low, hit)

    error = jnp.zeros((subset_count, padded), jnp.float32)
    update = jnp.zeros((padded, row_count), jnp.float32)
    for d in range(0, nz, 2):
        for i in (d, d + 1):
            if i > 0:
                pz_in[i](pred.at[far[i]])
                px_in.append(send(pred.at[far[i]], pred.at[far[i]], x_dev))
        error, update = use_pair((far[d], far[d + 1]), error, update)
    for arrive, row, col in ek_in:
        arrive(eig.at[row, col])
    whole_high, whole_low = split(eig[...].reshape(rows * subset_count, eig_ref.shape[1]))
    own_high, own_low = split(eig_ref[...] * scale_ref[...])
    metric = dot_nt(own_high, whole_high) + dot_nt(own_high, whole_low)
    metric_high, metric_low = split(metric + dot_nt(own_low, whole_high))
    for d in range(0, nz, 2):
        for i in (d, d + 1):
            px_in[i](pred.at[near[i]])
        error, update = use_pair((near[d], near[d + 1]), error, update)

    pack(error, eall.at[r])
    fz_in = [None] + [send(eall.at[r], eall.at[r], z_dev(d)) for d in range(1, nz)]
    fx_in = [send(eall.at[r], eall.at[r], x_dev)]
    upd[...] = coef - step_rate * update
    for d in range(1, nz):
        fz_in[d](eall.at[near[d]])
        fx_in.append(send(eall.at[near[d]], eall.at[near[d]], x_dev))
    for d in range(nz):
        fx_in[d](eall.at[far[d]])
    high, low = split(jnp.concatenate([unpack(eall.at[row]) for row in range(rows)], axis=0))
    correction = dot_nn(metric_high, high) + dot_nn(metric_high, low) + dot_nn(metric_low, high)
    high, low = split(jnp.transpose(correction))
    moved = dot_nn(high, pick_t) + dot_nn(low, pick_t)
    coef_ref[...] = (upd[...] + step_rate * moved)[0:class_count]
    leaving.append(pltpu.make_async_copy(coef_ref, new_hbm, local_sem.at[9 + rows]))
    leaving[-1].start()
    for copy in leaving:
        copy.wait()
    for copy in sent:
        copy.wait_send()


def fused_shards(
    rows, cls,
    centers, coefficients, batch_features, batch_labels, batch_index,
    subset_index, eigen_vectors, eigen_scale,
):
    row_count, width = centers.shape
    class_count = coefficients.shape[0]
    cols = batch_features.shape[0]
    subset_count, eig_count = eigen_vectors.shape
    padded = -(-class_count // 16) * 16
    nz = rows // NX
    copies = 13 * rows + 40
    f32, short = jnp.float32, jnp.int16
    hbm = pl.BlockSpec(memory_space=pltpu.HBM)
    return pl.pallas_call(
        functools.partial(fused_kernel, rows, cls, class_count),
        out_shape=(
            jax.ShapeDtypeStruct((class_count, rows * cols), f32),
            jax.ShapeDtypeStruct((class_count, row_count), f32),
        ),
        in_specs=[hbm] * 8,
        out_specs=(hbm, hbm),
        scratch_shapes=[
            pltpu.VMEM((rows, cls * width, cols), jnp.bfloat16),
            pltpu.VMEM((cls * width, row_count), jnp.bfloat16),
            pltpu.VMEM((rows, cls, subset_count // cls, eig_count), f32),
            pltpu.VMEM((rows, 2 * subset_count, cols), jnp.bfloat16),
            pltpu.VMEM((nz, padded + 16, cols), short),
            pltpu.VMEM((nz, padded + 16, cols), short),
            pltpu.VMEM((nz, padded, cols), f32),
            pltpu.VMEM((nz - 1, padded + 16, cols), short),
            pltpu.VMEM((nz - 1, padded + 16, cols), short),
            pltpu.VMEM((rows, padded + 16, cols), short),
            pltpu.VMEM((rows, subset_count + 16, padded), short),
            pltpu.VMEM((padded, row_count), f32),
            pltpu.VMEM((rows, class_count, cols), f32),
            pltpu.VMEM((class_count, row_count), f32),
            pltpu.VMEM((rows, cols), jnp.int32),
            pltpu.VMEM((rows, cols), jnp.int32),
            pltpu.VMEM((1, subset_count), jnp.int32),
            pltpu.VMEM((subset_count, eig_count), f32),
            pltpu.VMEM((1, eig_count), f32),
            pltpu.SemaphoreType.DMA((copies,)),
            pltpu.SemaphoreType.DMA((copies,)),
            pltpu.SemaphoreType.DMA((rows + 10,)),
        ],
        compiler_params=pltpu.CompilerParams(
            collective_id=0, has_side_effects=True, vmem_limit_bytes=62 * 1024 * 1024
        ),
    )(
        centers.T, coefficients, batch_features.T,
        batch_labels.reshape(rows, cols), batch_index.reshape(rows, cols),
        subset_index.reshape(1, subset_count), eigen_vectors,
        eigen_scale.reshape(1, eig_count),
    )


def plain_shards(
    centers, coefficients, batch_features, batch_labels, batch_index,
    subset_index, eigen_vectors, eigen_scale,
):
    row_count = centers.shape[0]
    first_row = lax.axis_index("rows") * row_count
    subset_local = subset_index - first_row
    batch_rows = lax.all_gather(batch_features, "rows", axis=0, tiled=True)
    batch_whole = lax.all_gather(batch_rows, "cls", axis=1, tiled=True)
    batch_norm = square_norm(batch_whole)
    center_whole = lax.all_gather(centers, "cls", axis=1, tiled=True)
    inner = jnp.einsum("cd,bd->cb", center_whole, batch_whole, preferred_element_type=jnp.float32)
    kernel_centers = kernel_block(
        inner, square_norm(center_whole)[:, None], batch_norm[None, :]
    )
    subset_kernel = kernel_centers[subset_local]
    partial_pred = jnp.dot(coefficients, kernel_centers, precision=HIGHEST)
    class_count = coefficients.shape[0]
    class_start = lax.axis_index("cls") * class_count
    class_ids = jnp.arange(class_count, dtype=jnp.int32) + class_start
    targets = (batch_labels[None, :] == class_ids[:, None]).astype(jnp.float32)
    basis_part = jnp.dot(eigen_vectors.T, subset_kernel, precision=HIGHEST)
    predicted, basis_sum = lax.psum((partial_pred, basis_part), "rows")
    gradient = predicted - targets
    projected = jnp.dot(gradient, basis_sum.T, precision=HIGHEST)
    correction = jnp.dot(
        projected * eigen_scale[None, :], eigen_vectors.T, precision=HIGHEST
    )
    batch_local = batch_index - first_row
    is_owned = (batch_local >= 0) & (batch_local < row_count)
    batch_slot = jnp.where(is_owned, batch_local, row_count)
    updated = coefficients.at[:, batch_slot].add(-step_rate * gradient, mode="drop")
    updated = updated.at[:, subset_local].add(step_rate * correction)
    return (predicted, updated)


def solution(mesh):
    rows, cls = mesh.shape["rows"], mesh.shape["cls"]

    def shards(*args):
        cols = args[2].shape[0]
        fits = rows % (2 * NX) == 0 and cls == 2 * NCORE and cols % 128 == 0
        if fits:
            return fused_shards(rows, cls, *args)
        return plain_shards(*args)

    return jax.shard_map(
        shards,
        mesh=mesh,
        in_specs=(
            P("rows", "cls"), P("cls", "rows"), P("rows", "cls"), P(), P(),
            P("rows"), P("rows", None), P(),
        ),
        out_specs=(P("cls", None), P("cls", "rows")),
        check_vma=False,
    )
```

```python
import functools

import jax
import jax.numpy as jnp
from jax import lax
from jax.experimental import pallas as pl
from jax.experimental.pallas import tpu as pltpu
from jax.sharding import PartitionSpec as P

spread = 4.0
step_rate = 0.5
HIGHEST = lax.Precision.HIGHEST
MESH = pl.DeviceIdType.MESH
NX = 2
NCORE = 2
LARGEST = 32767.0
STEPS = 256.0


def kernel_block(inner, row_norm, col_norm):
    squared = row_norm + col_norm - 2.0 * inner
    return jnp.exp(-jnp.sqrt(jnp.maximum(squared, 0.0)) / spread)


def square_norm(features):
    return jnp.sum(jnp.square(features.astype(jnp.float32)), axis=1)


def dot_nt(a, b):
    return lax.dot_general(
        a, b, (((1,), (1,)), ((), ())), preferred_element_type=jnp.float32
    )


def dot_nn(a, b):
    return jnp.dot(a, b, preferred_element_type=jnp.float32)


def split(value):
    high = value.astype(jnp.bfloat16)
    low = (value - high.astype(jnp.float32)).astype(jnp.bfloat16)
    return high, low


def pack(value, slot):
    count = value.shape[0]
    top = jnp.maximum(jnp.max(jnp.abs(value), axis=0, keepdims=True), 1e-37)
    code = jnp.clip(jnp.ceil(jnp.log2(top) * STEPS) + 1.0, -32000.0, 32000.0)
    gain = LARGEST * jnp.exp2(-code / STEPS)
    level = jnp.clip(jnp.round(value * gain), -LARGEST, LARGEST)
    slot[0:count, :] = level.astype(jnp.int32).astype(jnp.int16)
    codes = jnp.broadcast_to(code, (16, value.shape[1]))
    slot[count:count + 16, :] = codes.astype(jnp.int32).astype(jnp.int16)


def unpack(slot):
    count = slot.shape[0] - 16
    codes = slot[count:count + 16, :].astype(jnp.int32).astype(jnp.float32)
    unit = jnp.exp2(codes[0:1, :] / STEPS) / LARGEST
    return slot[0:count, :].astype(jnp.int32).astype(jnp.float32) * unit


def fused_kernel(
    rows, cls, class_count,
    cen_hbm, coef_hbm, bat_hbm, lab_hbm, idx_hbm, sub_hbm, eig_hbm, scale_hbm,
    pred_hbm, new_hbm,
    batch, cen, eig, sk, xsend, xrecv, acc, zsend, zrecv, pred, eall, upd,
    coef_ref, lab_ref, idx_ref, sub_ref, eig_ref, scale_ref,
    send_sem, recv_sem, local_sem,
):
    nz = rows // NX
    r = lax.axis_index("rows")
    c = lax.axis_index("cls")
    z, x = r // NX, r % NX
    y, k = c // NCORE, c % NCORE
    flip = 1 - 2 * x
    cy = (1 - y) * NCORE + k
    ck = y * NCORE + (1 - k)
    cyk = (1 - y) * NCORE + (1 - k)
    width, row_count = cen_hbm.shape
    cols = bat_hbm.shape[1]
    subset_count = eig_ref.shape[0]
    eig_part = subset_count // cls
    padded = upd.shape[0]
    first_row = r * row_count
    x_dev, y_dev, k_dev = (r + flip, c), (r, cy), (r, ck)
    near = [lax.rem(z + nz - d, nz) * NX + x for d in range(nz)]
    far = [row + flip for row in near]
    ahead = [lax.rem(z + d, nz) for d in range(nz)]

    def z_dev(d):
        return (ahead[d] * NX + x, c)

    barrier = pltpu.get_barrier_semaphore()
    partners = [x_dev, y_dev, k_dev] + [z_dev(d) for d in range(1, nz)]
    for dev in partners:
        pl.semaphore_signal(barrier, inc=1, device_id=dev, device_id_type=MESH)

    def part(col):
        return pl.ds(pl.multiple_of(col * width, width), width)

    eig_rows = pl.ds(pl.multiple_of(c * eig_part, eig_part), eig_part)
    own_eig = eig_hbm.at[eig_rows]
    local = [
        pltpu.make_async_copy(src, dst, local_sem.at[n])
        for n, (src, dst) in enumerate((
            (sub_hbm, sub_ref), (cen_hbm, cen.at[part(c)]), (bat_hbm, batch.at[r, part(c)]),
            (coef_hbm, coef_ref), (lab_hbm, lab_ref), (idx_hbm, idx_ref),
            (eig_hbm, eig_ref), (own_eig, eig.at[r, c]), (scale_hbm, scale_ref),
        ))
    ]
    for copy in local:
        copy.start()
    pl.semaphore_wait(barrier, len(partners))

    sent = []

    def send(src, dst, dev):
        n = len(sent)
        copy = pltpu.make_async_remote_copy(
            src_ref=src, dst_ref=dst, send_sem=send_sem.at[n], recv_sem=recv_sem.at[n],
            device_id=dev, device_id_type=MESH,
        )
        copy.start()
        sent.append(copy)

        def arrive(slot):
            pltpu.make_async_remote_copy(
                src_ref=slot, dst_ref=slot, send_sem=send_sem.at[n], recv_sem=recv_sem.at[n],
                device_id=dev, device_id_type=MESH,
            ).wait_recv()

        return arrive

    def slot(row, col):
        return batch.at[row, part(col)]

    def pass_on(row, col, dev):
        return send(slot(row, col), slot(row, col), dev)

    z_in = [None] + [send(bat_hbm, slot(r, c), z_dev(d)) for d in range(1, nz)]
    x_in = [send(bat_hbm, slot(r, c), x_dev)]
    y_in = [send(bat_hbm, slot(r, c), y_dev)]
    cen_y = send(cen_hbm, cen.at[part(c)], y_dev)
    near_in = [[send(bat_hbm, slot(r, c), k_dev)]]
    cen_k = send(cen_hbm, cen.at[part(c)], k_dev)

    for copy in local:
        copy.wait()
    coef = coef_ref[...]
    if padded > class_count:
        upd[...] = jnp.zeros_like(upd)
        upd[0:class_count, :] = coef
        coef = upd[...]
    coef_high, coef_low = split(coef)
    subset_local = sub_ref[...] - first_row
    pick_t = jnp.transpose(
        (
            lax.broadcasted_iota(jnp.int32, (row_count, subset_count), 0) == subset_local
        ).astype(jnp.float32)
    ).astype(jnp.bfloat16)
    for d in range(1, nz):
        z_in[d](slot(near[d], c))
        y_in.append(pass_on(near[d], c, y_dev))
        x_in.append(pass_on(near[d], c, x_dev))
        near_in.append([pass_on(near[d], c, k_dev)])
    cen_y(cen.at[part(cy)])
    cen_yk = send(cen.at[part(cy)], cen.at[part(cy)], k_dev)
    xy_in = []
    for d in range(nz):
        y_in[d](slot(near[d], cy))
        if d < nz - 1:
            xy_in.append(pass_on(near[d], cy, x_dev))
        near_in[d].append(pass_on(near[d], cy, k_dev))
    ez_in = [None] + [send(own_eig, eig.at[r, c], z_dev(d)) for d in range(1, nz)]
    far_in = [[] for _ in range(nz)]

    cen_k(cen.at[part(ck)])
    cen_yk(cen.at[part(cyk)])
    cen_wide = jnp.transpose(cen[...].astype(jnp.float32))
    cen_norm = jnp.sum(cen_wide * cen_wide, axis=1, keepdims=True)
    cen_rows = cen_wide.astype(jnp.bfloat16)

    later = []

    def part_pred(first, second):
        both = jnp.concatenate([batch[first], batch[second]], axis=1)
        wide = both.astype(jnp.float32)
        norm = jnp.sum(wide * wide, axis=0, keepdims=True)
        high, low = split(kernel_block(dot_nn(cen_rows, both), cen_norm, norm))
        later.append((first, second, high, low))
        return dot_nn(coef_high, high) + dot_nn(coef_high, low) + dot_nn(coef_low, high)

    def subset_part():
        for first, second, high, low in later:
            sk_high = dot_nn(pick_t, high).astype(jnp.bfloat16)
            sk_low = dot_nn(pick_t, low).astype(jnp.bfloat16)
            for at, row in enumerate((first, second)):
                lanes = slice(at * cols, (at + 1) * cols)
                sk[row, 0:subset_count, :] = sk_high[:, lanes]
                sk[row, subset_count:2 * subset_count, :] = sk_low[:, lanes]
        later.clear()

    for i in range(nz - 1, -1, -1):
        x_in[i](slot(far[i], c))
        if i == nz - 1:
            xy_in.append(pass_on(far[i], c, y_dev))
        far_in[i].append(pass_on(far[i], c, k_dev))
    sum_in = []
    for d in range(0, nz, 2):
        for i in (d, d + 1):
            near_in[i][0](slot(near[i], ck))
            near_in[i][1](slot(near[i], cyk))
        both = part_pred(near[d], near[d + 1])
        for at, i in enumerate((d, d + 1)):
            pack(both[:, at * cols:(at + 1) * cols], xsend.at[i])
            sum_in.append(send(xsend.at[i], xrecv.at[i], x_dev))
        subset_part()
        for i in (d, d + 1):
            xy_in[i](slot(far[i], cy))
            far_in[i].append(pass_on(far[i], cy, k_dev))
    ex_in = [send(own_eig, eig.at[r, c], x_dev)]
    for d in range(1, nz):
        ez_in[d](eig.at[near[d], c])
        ex_in.append(send(eig.at[near[d], c], eig.at[near[d], c], x_dev))
    for d in range(0, nz, 2):
        for i in (d, d + 1):
            far_in[i][0](slot(far[i], ck))
            far_in[i][1](slot(far[i], cyk))
        both = part_pred(far[d], far[d + 1])
        for at, i in enumerate((d, d + 1)):
            acc[i] = both[:, at * cols:(at + 1) * cols]

    rs_in = [None] * nz
    for d in range(1, nz):
        sum_in[d](xrecv.at[d])
        pack(acc[d] + unpack(xrecv.at[d]), zsend.at[d - 1])
        rs_in[d] = send(zsend.at[d - 1], zrecv.at[d - 1], z_dev(nz - d))
    sum_in[0](xrecv.at[0])
    total = acc[0] + unpack(xrecv.at[0])
    subset_part()

    ey_in, ek_in = [], []

    def eig_on(row):
        ey_in.append((send(eig.at[row, c], eig.at[row, c], y_dev), row))
        ek_in.append((send(eig.at[row, c], eig.at[row, c], k_dev), row, ck))

    for row in near:
        eig_on(row)
    for d in range(1, nz):
        rs_in[d](zrecv.at[d - 1])
        total += unpack(zrecv.at[d - 1])
    mine = far[0]
    pack(total, pred.at[mine])

    pz_in = [None] + [send(pred.at[mine], pred.at[mine], z_dev(d)) for d in range(1, nz)]
    px_in = [send(pred.at[mine], pred.at[mine], x_dev)]

    for arrive, row in zip(ex_in, far):
        arrive(eig.at[row, c])
        eig_on(row)

    class_ids = lax.broadcasted_iota(jnp.int32, (padded, cols), 0) + c * class_count
    center_ids = lax.broadcasted_iota(jnp.int32, (row_count, cols), 0) + first_row

    leaving = []

    def use_pair(pair, error):
        grads, hits, kernels = [], [], []
        for row in pair:
            columns = pl.ds(pl.multiple_of(row * cols, cols), cols)
            n = 9 + len(leaving)
            leaving.append(
                pltpu.make_async_copy(pred.at[row], pred_hbm.at[:, columns], local_sem.at[n])
            )
            leaving[-1].start()
            value = unpack(pred.at[row])
            grads.append(value - (lab_ref[pl.ds(row, 1), :] == class_ids).astype(jnp.float32))
            kernels.append(sk[row])
        high, low = split(jnp.concatenate(grads, axis=1))
        kernel_pair = jnp.concatenate(kernels, axis=1)
        two = dot_nt(kernel_pair, high)
        error += two[0:subset_count] + two[subset_count:]
        return error + dot_nt(kernel_pair[0:subset_count], low), (pair, high, low)

    def scatter(update, moves):
        for pair, high, low in moves:
            hit = jnp.concatenate(
                [(idx_ref[pl.ds(row, 1), :] == center_ids).astype(jnp.float32) for row in pair],
                axis=1,
            ).astype(jnp.bfloat16)
            update += dot_nt(high, hit) + dot_nt(low, hit)
        return update

    error = jnp.zeros((subset_count, padded), jnp.float32)
    update = jnp.zeros((padded, row_count), jnp.float32)
    for d in range(0, nz, 2):
        for i in (d, d + 1):
            if i > 0:
                pz_in[i](pred.at[far[i]])
                px_in.append(send(pred.at[far[i]], pred.at[far[i]], x_dev))
        error, move = use_pair((far[d], far[d + 1]), error)
        update = scatter(update, [move])
    moves = []
    for d in range(0, nz, 2):
        for i in (d, d + 1):
            px_in[i](pred.at[near[i]])
        error, move = use_pair((near[d], near[d + 1]), error)
        moves.append(move)

    pack(error, eall.at[r])
    fz_in = [None] + [send(eall.at[r], eall.at[r], z_dev(d)) for d in range(1, nz)]
    fx_in = [send(eall.at[r], eall.at[r], x_dev)]
    for arrive, row in ey_in:
        arrive(eig.at[row, cy])
        ek_in.append((send(eig.at[row, cy], eig.at[row, cy], k_dev), row, cyk))
    upd[...] = coef - step_rate * scatter(update, moves[:1])
    for d in range(1, nz):
        fz_in[d](eall.at[near[d]])
        fx_in.append(send(eall.at[near[d]], eall.at[near[d]], x_dev))
    upd[...] -= step_rate * scatter(jnp.zeros_like(update), moves[1:])
    for arrive, row, col in ek_in:
        arrive(eig.at[row, col])
    whole_high, whole_low = split(eig[...].reshape(rows * subset_count, eig_ref.shape[1]))
    own_high, own_low = split(eig_ref[...] * scale_ref[...])
    metric = dot_nt(own_high, whole_high) + dot_nt(own_high, whole_low)
    metric_high, metric_low = split(metric + dot_nt(own_low, whole_high))
    for d in range(nz):
        fx_in[d](eall.at[far[d]])
    high, low = split(jnp.concatenate([unpack(eall.at[row]) for row in range(rows)], axis=0))
    correction = dot_nn(metric_high, high) + dot_nn(metric_high, low) + dot_nn(metric_low, high)
    high, low = split(jnp.transpose(correction))
    moved = dot_nn(high, pick_t) + dot_nn(low, pick_t)
    coef_ref[...] = (upd[...] + step_rate * moved)[0:class_count]
    leaving.append(pltpu.make_async_copy(coef_ref, new_hbm, local_sem.at[9 + rows]))
    leaving[-1].start()
    for copy in leaving:
        copy.wait()
    for copy in sent:
        copy.wait_send()


def fused_shards(
    rows, cls,
    centers, coefficients, batch_features, batch_labels, batch_index,
    subset_index, eigen_vectors, eigen_scale,
):
    row_count, width = centers.shape
    class_count = coefficients.shape[0]
    cols = batch_features.shape[0]
    subset_count, eig_count = eigen_vectors.shape
    padded = -(-class_count // 16) * 16
    nz = rows // NX
    copies = 13 * rows + 40
    f32, short = jnp.float32, jnp.int16
    hbm = pl.BlockSpec(memory_space=pltpu.HBM)
    levels, updated = pl.pallas_call(
        functools.partial(fused_kernel, rows, cls, class_count),
        out_shape=(
            jax.ShapeDtypeStruct((padded + 16, rows * cols), short),
            jax.ShapeDtypeStruct((class_count, row_count), f32),
        ),
        in_specs=[hbm] * 8,
        out_specs=(hbm, hbm),
        scratch_shapes=[
            pltpu.VMEM((rows, cls * width, cols), jnp.bfloat16),
            pltpu.VMEM((cls * width, row_count), jnp.bfloat16),
            pltpu.VMEM((rows, cls, subset_count // cls, eig_count), f32),
            pltpu.VMEM((rows, 2 * subset_count, cols), jnp.bfloat16),
            pltpu.VMEM((nz, padded + 16, cols), short),
            pltpu.VMEM((nz, padded + 16, cols), short),
            pltpu.VMEM((nz, padded, cols), f32),
            pltpu.VMEM((nz - 1, padded + 16, cols), short),
            pltpu.VMEM((nz - 1, padded + 16, cols), short),
            pltpu.VMEM((rows, padded + 16, cols), short),
            pltpu.VMEM((rows, subset_count + 16, padded), short),
            pltpu.VMEM((padded, row_count), f32),
            pltpu.VMEM((class_count, row_count), f32),
            pltpu.VMEM((rows, cols), jnp.int32),
            pltpu.VMEM((rows, cols), jnp.int32),
            pltpu.VMEM((1, subset_count), jnp.int32),
            pltpu.VMEM((subset_count, eig_count), f32),
            pltpu.VMEM((1, eig_count), f32),
            pltpu.SemaphoreType.DMA((copies,)),
            pltpu.SemaphoreType.DMA((copies,)),
            pltpu.SemaphoreType.DMA((rows + 10,)),
        ],
        compiler_params=pltpu.CompilerParams(
            collective_id=0, has_side_effects=True, vmem_limit_bytes=62 * 1024 * 1024
        ),
    )(
        centers.T, coefficients, batch_features.T,
        batch_labels.reshape(rows, cols), batch_index.reshape(rows, cols),
        subset_index.reshape(1, subset_count), eigen_vectors,
        eigen_scale.reshape(1, eig_count),
    )
    unit = jnp.exp2(levels[padded:padded + 1].astype(f32) / STEPS) / LARGEST
    return levels[0:class_count].astype(f32) * unit, updated


def plain_shards(
    centers, coefficients, batch_features, batch_labels, batch_index,
    subset_index, eigen_vectors, eigen_scale,
):
    row_count = centers.shape[0]
    first_row = lax.axis_index("rows") * row_count
    subset_local = subset_index - first_row
    batch_rows = lax.all_gather(batch_features, "rows", axis=0, tiled=True)
    batch_whole = lax.all_gather(batch_rows, "cls", axis=1, tiled=True)
    batch_norm = square_norm(batch_whole)
    center_whole = lax.all_gather(centers, "cls", axis=1, tiled=True)
    inner = jnp.einsum("cd,bd->cb", center_whole, batch_whole, preferred_element_type=jnp.float32)
    kernel_centers = kernel_block(
        inner, square_norm(center_whole)[:, None], batch_norm[None, :]
    )
    subset_kernel = kernel_centers[subset_local]
    partial_pred = jnp.dot(coefficients, kernel_centers, precision=HIGHEST)
    class_count = coefficients.shape[0]
    class_start = lax.axis_index("cls") * class_count
    class_ids = jnp.arange(class_count, dtype=jnp.int32) + class_start
    targets = (batch_labels[None, :] == class_ids[:, None]).astype(jnp.float32)
    basis_part = jnp.dot(eigen_vectors.T, subset_kernel, precision=HIGHEST)
    predicted, basis_sum = lax.psum((partial_pred, basis_part), "rows")
    gradient = predicted - targets
    projected = jnp.dot(gradient, basis_sum.T, precision=HIGHEST)
    correction = jnp.dot(
        projected * eigen_scale[None, :], eigen_vectors.T, precision=HIGHEST
    )
    batch_local = batch_index - first_row
    is_owned = (batch_local >= 0) & (batch_local < row_count)
    batch_slot = jnp.where(is_owned, batch_local, row_count)
    updated = coefficients.at[:, batch_slot].add(-step_rate * gradient, mode="drop")
    updated = updated.at[:, subset_local].add(step_rate * correction)
    return (predicted, updated)


def solution(mesh):
    rows, cls = mesh.shape["rows"], mesh.shape["cls"]

    def shards(*args):
        cols = args[2].shape[0]
        fits = rows % (2 * NX) == 0 and cls == 2 * NCORE and cols % 128 == 0
        if fits:
            return fused_shards(rows, cls, *args)
        return plain_shards(*args)

    return jax.shard_map(
        shards,
        mesh=mesh,
        in_specs=(
            P("rows", "cls"), P("cls", "rows"), P("rows", "cls"), P(), P(),
            P("rows"), P("rows", None), P(),
        ),
        out_specs=(P("cls", None), P("cls", "rows")),
        check_vma=False,
    )
```

```python
import functools

import jax
import jax.numpy as jnp
from jax import lax
from jax.experimental import pallas as pl
from jax.experimental.pallas import tpu as pltpu
from jax.sharding import PartitionSpec as P

spread = 4.0
step_rate = 0.5
HIGHEST = lax.Precision.HIGHEST
MESH = pl.DeviceIdType.MESH
NX = 2
NCORE = 2
LARGEST = 32767.0
STEPS = 256.0


def kernel_block(inner, row_norm, col_norm):
    squared = row_norm + col_norm - 2.0 * inner
    return jnp.exp(-jnp.sqrt(jnp.maximum(squared, 0.0)) / spread)


def square_norm(features):
    return jnp.sum(jnp.square(features.astype(jnp.float32)), axis=1)


def dot_nt(a, b):
    return lax.dot_general(
        a, b, (((1,), (1,)), ((), ())), preferred_element_type=jnp.float32
    )


def dot_nn(a, b):
    return jnp.dot(a, b, preferred_element_type=jnp.float32)


def split(value):
    high = value.astype(jnp.bfloat16)
    low = (value - high.astype(jnp.float32)).astype(jnp.bfloat16)
    return high, low


def pack(value, slot):
    count = value.shape[0]
    top = jnp.maximum(jnp.max(jnp.abs(value), axis=0, keepdims=True), 1e-37)
    code = jnp.clip(jnp.ceil(jnp.log2(top) * STEPS) + 1.0, -32000.0, 32000.0)
    gain = LARGEST * jnp.exp2(-code / STEPS)
    level = jnp.clip(jnp.round(value * gain), -LARGEST, LARGEST)
    slot[0:count, :] = level.astype(jnp.int32).astype(jnp.int16)
    codes = jnp.broadcast_to(code, (16, value.shape[1]))
    slot[count:count + 16, :] = codes.astype(jnp.int32).astype(jnp.int16)


def unpack(slot):
    count = slot.shape[0] - 16
    codes = slot[count:count + 16, :].astype(jnp.int32).astype(jnp.float32)
    unit = jnp.exp2(codes[0:1, :] / STEPS) / LARGEST
    return slot[0:count, :].astype(jnp.int32).astype(jnp.float32) * unit


def fused_kernel(
    rows, cls, class_count,
    cen_hbm, coef_hbm, bat_hbm, lab_hbm, idx_hbm, sub_hbm, eig_hbm, scale_hbm,
    pred_hbm, new_hbm,
    batch, cen, eig, sk, sk_own, skq, pick, xsend, xrecv, acc, zsend, zrecv, pred, upd,
    pred_ref, coef_ref, lab_ref, idx_ref, sub_ref, eig_ref, scale_ref,
    send_sem, recv_sem, local_sem,
):
    nz = rows // NX
    r = lax.axis_index("rows")
    c = lax.axis_index("cls")
    z, x = r // NX, r % NX
    y, k = c // NCORE, c % NCORE
    flip = 1 - 2 * x
    cy = (1 - y) * NCORE + k
    ck = y * NCORE + (1 - k)
    cyk = (1 - y) * NCORE + (1 - k)
    width, row_count = cen_hbm.shape
    cols = bat_hbm.shape[1]
    subset_count = eig_ref.shape[0]
    eig_part = subset_count // cls
    padded = upd.shape[0]
    first_row = r * row_count
    x_dev, y_dev, k_dev = (r + flip, c), (r, cy), (r, ck)
    near = [lax.rem(z + nz - d, nz) * NX + x for d in range(nz)]
    far = [row + flip for row in near]
    ahead = [lax.rem(z + d, nz) for d in range(nz)]

    def z_dev(d):
        return (ahead[d] * NX + x, c)

    barrier = pltpu.get_barrier_semaphore()
    partners = [x_dev, y_dev, k_dev] + [z_dev(d) for d in range(1, nz)]
    for dev in partners:
        pl.semaphore_signal(barrier, inc=1, device_id=dev, device_id_type=MESH)

    def part(col):
        return pl.ds(pl.multiple_of(col * width, width), width)

    eig_rows = pl.ds(pl.multiple_of(c * eig_part, eig_part), eig_part)
    own_eig = eig_hbm.at[eig_rows]
    local = [
        pltpu.make_async_copy(src, dst, local_sem.at[n])
        for n, (src, dst) in enumerate((
            (sub_hbm, sub_ref), (cen_hbm, cen.at[part(c)]), (bat_hbm, batch.at[r, part(c)]),
            (coef_hbm, coef_ref), (lab_hbm, lab_ref), (idx_hbm, idx_ref),
            (eig_hbm, eig_ref), (own_eig, eig.at[r, c]), (scale_hbm, scale_ref),
        ))
    ]
    for copy in local:
        copy.start()
    pl.semaphore_wait(barrier, len(partners))

    sent = []

    def send(src, dst, dev):
        n = len(sent)
        copy = pltpu.make_async_remote_copy(
            src_ref=src, dst_ref=dst, send_sem=send_sem.at[n], recv_sem=recv_sem.at[n],
            device_id=dev, device_id_type=MESH,
        )
        copy.start()
        sent.append(copy)

        def arrive(slot):
            pltpu.make_async_remote_copy(
                src_ref=slot, dst_ref=slot, send_sem=send_sem.at[n], recv_sem=recv_sem.at[n],
                device_id=dev, device_id_type=MESH,
            ).wait_recv()

        return arrive

    def slot(row, col):
        return batch.at[row, part(col)]

    def pass_on(row, col, dev):
        return send(slot(row, col), slot(row, col), dev)

    z_in = [None] + [send(bat_hbm, slot(r, c), z_dev(d)) for d in range(1, nz)]
    x_in = [send(bat_hbm, slot(r, c), x_dev)]
    y_in = [send(bat_hbm, slot(r, c), y_dev)]
    cen_y = send(cen_hbm, cen.at[part(c)], y_dev)
    near_in = [[send(bat_hbm, slot(r, c), k_dev)]]
    cen_k = send(cen_hbm, cen.at[part(c)], k_dev)

    for copy in local:
        copy.wait()
    coef = coef_ref[...]
    if padded > class_count:
        upd[...] = jnp.zeros_like(upd)
        upd[0:class_count, :] = coef
        coef = upd[...]
    coef_high, coef_low = split(coef)
    subset_local = sub_ref[...] - first_row
    pick_t = jnp.transpose(
        (
            lax.broadcasted_iota(jnp.int32, (row_count, subset_count), 0) == subset_local
        ).astype(jnp.float32)
    ).astype(jnp.bfloat16)
    for d in range(1, nz):
        z_in[d](slot(near[d], c))
        y_in.append(pass_on(near[d], c, y_dev))
        x_in.append(pass_on(near[d], c, x_dev))
        near_in.append([pass_on(near[d], c, k_dev)])
    cen_y(cen.at[part(cy)])
    cen_yk = send(cen.at[part(cy)], cen.at[part(cy)], k_dev)
    xy_in = []
    for d in range(nz):
        y_in[d](slot(near[d], cy))
        if d < nz - 1:
            xy_in.append(pass_on(near[d], cy, x_dev))
        near_in[d].append(pass_on(near[d], cy, k_dev))
    ez_in = [None] + [send(own_eig, eig.at[r, c], z_dev(d)) for d in range(1, nz)]
    far_in = [[] for _ in range(nz)]

    cen_k(cen.at[part(ck)])
    cen_yk(cen.at[part(cyk)])
    cen_wide = jnp.transpose(cen[...].astype(jnp.float32))
    cen_norm = jnp.sum(cen_wide * cen_wide, axis=1, keepdims=True)
    cen_rows = cen_wide.astype(jnp.bfloat16)

    later = []
    pick[...] = pick_t
    pick_own = pick[eig_rows, :]

    def part_pred(first, second):
        both = jnp.concatenate([batch[first], batch[second]], axis=1)
        wide = both.astype(jnp.float32)
        norm = jnp.sum(wide * wide, axis=0, keepdims=True)
        high, low = split(kernel_block(dot_nn(cen_rows, both), cen_norm, norm))
        later.append((first, second, high, low))
        return dot_nn(coef_high, high) + dot_nn(coef_high, low) + dot_nn(coef_low, high)

    def subset_part():
        for first, second, high, low in later:
            both = dot_nn(pick_own, high) + dot_nn(pick_own, low)
            for at, row in enumerate((first, second)):
                sk_own[row] = both[:, at * cols:(at + 1) * cols]
        later.clear()

    for i in range(nz - 1, -1, -1):
        x_in[i](slot(far[i], c))
        if i == nz - 1:
            xy_in.append(pass_on(far[i], c, y_dev))
        far_in[i].append(pass_on(far[i], c, k_dev))
    sum_in = []
    for d in range(0, nz, 2):
        for i in (d, d + 1):
            near_in[i][0](slot(near[i], ck))
            near_in[i][1](slot(near[i], cyk))
        both = part_pred(near[d], near[d + 1])
        for at, i in enumerate((d, d + 1)):
            pack(both[:, at * cols:(at + 1) * cols], xsend.at[i])
            sum_in.append(send(xsend.at[i], xrecv.at[i], x_dev))
        subset_part()
        for i in (d, d + 1):
            xy_in[i](slot(far[i], cy))
            far_in[i].append(pass_on(far[i], cy, k_dev))
    ey_in, ek_in = [], []

    def eig_on(row):
        ey_in.append((send(eig.at[row, c], eig.at[row, c], y_dev), row))
        ek_in.append((send(eig.at[row, c], eig.at[row, c], k_dev), row, ck))

    eig_on(r)
    ex_in = [send(own_eig, eig.at[r, c], x_dev)]
    for d in range(1, nz):
        ez_in[d](eig.at[near[d], c])
        ex_in.append(send(eig.at[near[d], c], eig.at[near[d], c], x_dev))
        eig_on(near[d])
    for d in range(0, nz, 2):
        for i in (d, d + 1):
            far_in[i][0](slot(far[i], ck))
            far_in[i][1](slot(far[i], cyk))
        both = part_pred(far[d], far[d + 1])
        for at, i in enumerate((d, d + 1)):
            acc[i] = both[:, at * cols:(at + 1) * cols]

    rs_in = [None] * nz
    for d in range(1, nz):
        sum_in[d](xrecv.at[d])
        pack(acc[d] + unpack(xrecv.at[d]), zsend.at[d - 1])
        rs_in[d] = send(zsend.at[d - 1], zrecv.at[d - 1], z_dev(nz - d))
    sum_in[0](xrecv.at[0])
    total = acc[0] + unpack(xrecv.at[0])
    subset_part()

    values = jnp.concatenate([sk_own[row] for row in range(rows)], axis=1)
    top = jnp.maximum(jnp.max(values, axis=1, keepdims=True), 1e-37)
    code = jnp.clip(jnp.ceil(jnp.log2(top) * STEPS) + 1.0, -32000.0, 32000.0)
    level = jnp.clip(jnp.round(values * (LARGEST * jnp.exp2(-code / STEPS))), -LARGEST, LARGEST)
    level = level.astype(jnp.int32).astype(jnp.int16)
    for row in range(rows):
        skq[r, c, row] = level[:, row * cols:(row + 1) * cols]
    codes = jnp.broadcast_to(code, (eig_part, cols))
    skq[r, c, rows] = codes.astype(jnp.int32).astype(jnp.int16)

    def kern_on(row, col, dev):
        return send(skq.at[row, col], skq.at[row, col], dev)

    kz_in = [None] + [kern_on(r, c, z_dev(d)) for d in range(1, nz)]
    kx_in = [kern_on(r, c, x_dev)]
    ky_in = [(kern_on(r, c, y_dev), r)]
    kk_in = [(kern_on(r, c, k_dev), r, ck)]

    for d in range(1, nz):
        rs_in[d](zrecv.at[d - 1])
        total += unpack(zrecv.at[d - 1])
    mine = far[0]
    pack(total, pred.at[mine])

    pz_in = [None] + [send(pred.at[mine], pred.at[mine], z_dev(d)) for d in range(1, nz)]
    px_in = [send(pred.at[mine], pred.at[mine], x_dev)]

    for d in range(1, nz):
        kz_in[d](skq.at[near[d], c])
        kx_in.append(kern_on(near[d], c, x_dev))
        ky_in.append((kern_on(near[d], c, y_dev), near[d]))
        kk_in.append((kern_on(near[d], c, k_dev), near[d], ck))
    for arrive, row in zip(ex_in, far):
        arrive(eig.at[row, c])
        eig_on(row)
    for i in range(1, nz):
        pz_in[i](pred.at[far[i]])
        px_in.append(send(pred.at[far[i]], pred.at[far[i]], x_dev))
    for arrive, row in zip(kx_in, far):
        arrive(skq.at[row, c])
        ky_in.append((kern_on(row, c, y_dev), row))
        kk_in.append((kern_on(row, c, k_dev), row, ck))
    for arrive, row in ey_in:
        arrive(eig.at[row, cy])
        ek_in.append((send(eig.at[row, cy], eig.at[row, cy], k_dev), row, cyk))
    for arrive, row in ky_in:
        arrive(skq.at[row, cy])
        kk_in.append((kern_on(row, cy, k_dev), row, cyk))
    for arrive, row, col in ek_in:
        arrive(eig.at[row, col])
    whole_high, whole_low = split(eig[...].reshape(rows * subset_count, eig_ref.shape[1]))
    own_high, own_low = split(eig_ref[...] * scale_ref[...])
    metric = dot_nt(own_high, whole_high) + dot_nt(own_high, whole_low)
    metric_high, metric_low = split(metric + dot_nt(own_low, whole_high))
    for arrive, row, col in kk_in:
        arrive(skq.at[row, col])
    flat = (rows * subset_count, cols)
    units = skq[:, :, rows].astype(jnp.int32).astype(jnp.float32).reshape(flat)
    units = jnp.exp2(units / STEPS) / LARGEST
    for row in range(rows):
        levels = skq[:, :, row].astype(jnp.int32).astype(jnp.float32).reshape(flat)
        high, low = split(levels * units)
        mixed = dot_nn(metric_high, high) + dot_nn(metric_high, low) + dot_nn(metric_low, high)
        high, low = split(mixed)
        sk[row, 0:subset_count, :] = high
        sk[row, subset_count:2 * subset_count, :] = low

    class_ids = lax.broadcasted_iota(jnp.int32, (padded, cols), 0) + c * class_count
    center_ids = lax.broadcasted_iota(jnp.int32, (row_count, cols), 0) + first_row

    leaving = []

    def use_pair(pair, error):
        grads, hits, kernels = [], [], []
        for row in pair:
            columns = pl.ds(pl.multiple_of(row * cols, cols), cols)
            n = 9 + len(leaving)
            leaving.append(
                pltpu.make_async_copy(pred_ref.at[row], pred_hbm.at[:, columns], local_sem.at[n])
            )
            value = unpack(pred.at[row])
            pred_ref[row] = value[0:class_count]
            leaving[-1].start()
            grads.append(value - (lab_ref[pl.ds(row, 1), :] == class_ids).astype(jnp.float32))
            kernels.append(sk[row])
        high, low = split(jnp.concatenate(grads, axis=1))
        kernel_pair = jnp.concatenate(kernels, axis=1)
        two = dot_nt(kernel_pair, high)
        error += two[0:subset_count] + two[subset_count:]
        return error + dot_nt(kernel_pair[0:subset_count], low), (pair, high, low)

    def scatter(update, moves):
        for pair, high, low in moves:
            hit = jnp.concatenate(
                [(idx_ref[pl.ds(row, 1), :] == center_ids).astype(jnp.float32) for row in pair],
                axis=1,
            ).astype(jnp.bfloat16)
            update += dot_nt(high, hit) + dot_nt(low, hit)
        return update

    error = jnp.zeros((subset_count, padded), jnp.float32)
    update = jnp.zeros((padded, row_count), jnp.float32)
    for d in range(0, nz, 2):
        error, move = use_pair((far[d], far[d + 1]), error)
        update = scatter(update, [move])
    moves = []
    for d in range(0, nz, 2):
        for i in (d, d + 1):
            px_in[i](pred.at[near[i]])
        error, move = use_pair((near[d], near[d + 1]), error)
        moves.append(move)

    upd[...] = coef - step_rate * scatter(update, moves)
    high, low = split(jnp.transpose(error))
    moved = dot_nn(high, pick_t) + dot_nn(low, pick_t)
    coef_ref[...] = (upd[...] + step_rate * moved)[0:class_count]
    leaving.append(pltpu.make_async_copy(coef_ref, new_hbm, local_sem.at[9 + rows]))
    leaving[-1].start()
    for copy in leaving:
        copy.wait()
    for copy in sent:
        copy.wait_send()


def fused_shards(
    rows, cls,
    centers, coefficients, batch_features, batch_labels, batch_index,
    subset_index, eigen_vectors, eigen_scale,
):
    row_count, width = centers.shape
    class_count = coefficients.shape[0]
    cols = batch_features.shape[0]
    subset_count, eig_count = eigen_vectors.shape
    padded = -(-class_count // 16) * 16
    nz = rows // NX
    copies = 16 * rows + 40
    f32, short = jnp.float32, jnp.int16
    hbm = pl.BlockSpec(memory_space=pltpu.HBM)
    return pl.pallas_call(
        functools.partial(fused_kernel, rows, cls, class_count),
        out_shape=(
            jax.ShapeDtypeStruct((class_count, rows * cols), f32),
            jax.ShapeDtypeStruct((class_count, row_count), f32),
        ),
        in_specs=[hbm] * 8,
        out_specs=(hbm, hbm),
        scratch_shapes=[
            pltpu.VMEM((rows, cls * width, cols), jnp.bfloat16),
            pltpu.VMEM((cls * width, row_count), jnp.bfloat16),
            pltpu.VMEM((rows, cls, subset_count // cls, eig_count), f32),
            pltpu.VMEM((rows, 2 * subset_count, cols), jnp.bfloat16),
            pltpu.VMEM((rows, subset_count // cls, cols), f32),
            pltpu.VMEM((rows, cls, rows + 1, subset_count // cls, cols), short),
            pltpu.VMEM((subset_count, row_count), jnp.bfloat16),
            pltpu.VMEM((nz, padded + 16, cols), short),
            pltpu.VMEM((nz, padded + 16, cols), short),
            pltpu.VMEM((nz, padded, cols), f32),
            pltpu.VMEM((nz - 1, padded + 16, cols), short),
            pltpu.VMEM((nz - 1, padded + 16, cols), short),
            pltpu.VMEM((rows, padded + 16, cols), short),
            pltpu.VMEM((padded, row_count), f32),
            pltpu.VMEM((rows, class_count, cols), f32),
            pltpu.VMEM((class_count, row_count), f32),
            pltpu.VMEM((rows, cols), jnp.int32),
            pltpu.VMEM((rows, cols), jnp.int32),
            pltpu.VMEM((1, subset_count), jnp.int32),
            pltpu.VMEM((subset_count, eig_count), f32),
            pltpu.VMEM((1, eig_count), f32),
            pltpu.SemaphoreType.DMA((copies,)),
            pltpu.SemaphoreType.DMA((copies,)),
            pltpu.SemaphoreType.DMA((rows + 10,)),
        ],
        compiler_params=pltpu.CompilerParams(
            collective_id=0, has_side_effects=True, vmem_limit_bytes=62 * 1024 * 1024
        ),
    )(
        centers.T, coefficients, batch_features.T,
        batch_labels.reshape(rows, cols), batch_index.reshape(rows, cols),
        subset_index.reshape(1, subset_count), eigen_vectors,
        eigen_scale.reshape(1, eig_count),
    )


def plain_shards(
    centers, coefficients, batch_features, batch_labels, batch_index,
    subset_index, eigen_vectors, eigen_scale,
):
    row_count = centers.shape[0]
    first_row = lax.axis_index("rows") * row_count
    subset_local = subset_index - first_row
    batch_rows = lax.all_gather(batch_features, "rows", axis=0, tiled=True)
    batch_whole = lax.all_gather(batch_rows, "cls", axis=1, tiled=True)
    batch_norm = square_norm(batch_whole)
    center_whole = lax.all_gather(centers, "cls", axis=1, tiled=True)
    inner = jnp.einsum("cd,bd->cb", center_whole, batch_whole, preferred_element_type=jnp.float32)
    kernel_centers = kernel_block(
        inner, square_norm(center_whole)[:, None], batch_norm[None, :]
    )
    subset_kernel = kernel_centers[subset_local]
    partial_pred = jnp.dot(coefficients, kernel_centers, precision=HIGHEST)
    class_count = coefficients.shape[0]
    class_start = lax.axis_index("cls") * class_count
    class_ids = jnp.arange(class_count, dtype=jnp.int32) + class_start
    targets = (batch_labels[None, :] == class_ids[:, None]).astype(jnp.float32)
    basis_part = jnp.dot(eigen_vectors.T, subset_kernel, precision=HIGHEST)
    predicted, basis_sum = lax.psum((partial_pred, basis_part), "rows")
    gradient = predicted - targets
    projected = jnp.dot(gradient, basis_sum.T, precision=HIGHEST)
    correction = jnp.dot(
        projected * eigen_scale[None, :], eigen_vectors.T, precision=HIGHEST
    )
    batch_local = batch_index - first_row
    is_owned = (batch_local >= 0) & (batch_local < row_count)
    batch_slot = jnp.where(is_owned, batch_local, row_count)
    updated = coefficients.at[:, batch_slot].add(-step_rate * gradient, mode="drop")
    updated = updated.at[:, subset_local].add(step_rate * correction)
    return (predicted, updated)


def solution(mesh):
    rows, cls = mesh.shape["rows"], mesh.shape["cls"]

    def shards(*args):
        cols = args[2].shape[0]
        fits = rows % (2 * NX) == 0 and cls == 2 * NCORE and cols % 128 == 0
        if fits:
            return fused_shards(rows, cls, *args)
        return plain_shards(*args)

    return jax.shard_map(
        shards,
        mesh=mesh,
        in_specs=(
            P("rows", "cls"), P("cls", "rows"), P("rows", "cls"), P(), P(),
            P("rows"), P("rows", None), P(),
        ),
        out_specs=(P("cls", None), P("cls", "rows")),
        check_vma=False,
    )
```

```python
import functools

import jax
import jax.numpy as jnp
from jax import lax
from jax.experimental import pallas as pl
from jax.experimental.pallas import tpu as pltpu
from jax.sharding import PartitionSpec as P

spread = 4.0
step_rate = 0.5
HIGHEST = lax.Precision.HIGHEST
MESH = pl.DeviceIdType.MESH
NX = 2
NCORE = 2
LARGEST = 32767.0
STEPS = 256.0


def kernel_block(inner, row_norm, col_norm):
    squared = row_norm + col_norm - 2.0 * inner
    return jnp.exp(-jnp.sqrt(jnp.maximum(squared, 0.0)) / spread)


def square_norm(features):
    return jnp.sum(jnp.square(features.astype(jnp.float32)), axis=1)


def dot_nt(a, b):
    return lax.dot_general(
        a, b, (((1,), (1,)), ((), ())), preferred_element_type=jnp.float32
    )


def dot_nn(a, b):
    return jnp.dot(a, b, preferred_element_type=jnp.float32)


def split(value):
    high = value.astype(jnp.bfloat16)
    low = (value - high.astype(jnp.float32)).astype(jnp.bfloat16)
    return high, low


def pack(value, slot):
    count = value.shape[0]
    top = jnp.maximum(jnp.max(jnp.abs(value), axis=0, keepdims=True), 1e-37)
    code = jnp.clip(jnp.ceil(jnp.log2(top) * STEPS) + 1.0, -32000.0, 32000.0)
    gain = LARGEST * jnp.exp2(-code / STEPS)
    level = jnp.clip(jnp.round(value * gain), -LARGEST, LARGEST)
    slot[0:count, :] = level.astype(jnp.int32).astype(jnp.int16)
    codes = jnp.broadcast_to(code, (16, value.shape[1]))
    slot[count:count + 16, :] = codes.astype(jnp.int32).astype(jnp.int16)


def unpack(slot):
    count = slot.shape[0] - 16
    codes = slot[count:count + 16, :].astype(jnp.int32).astype(jnp.float32)
    unit = jnp.exp2(codes[0:1, :] / STEPS) / LARGEST
    return slot[0:count, :].astype(jnp.int32).astype(jnp.float32) * unit


def fused_kernel(
    rows, cls, class_count,
    cen_hbm, coef_hbm, bat_hbm, lab_hbm, idx_hbm, sub_hbm, eig_hbm, scale_hbm,
    pred_hbm, new_hbm,
    batch, cen, eig, sk, sk_own, skq, pick, xsend, xrecv, acc, zsend, zrecv, pred, upd,
    pred_ref, coef_ref, lab_ref, idx_ref, sub_ref, eig_ref, scale_ref,
    send_sem, recv_sem, local_sem,
):
    nz = rows // NX
    r = lax.axis_index("rows")
    c = lax.axis_index("cls")
    z, x = r // NX, r % NX
    y, k = c // NCORE, c % NCORE
    flip = 1 - 2 * x
    cy = (1 - y) * NCORE + k
    ck = y * NCORE + (1 - k)
    cyk = (1 - y) * NCORE + (1 - k)
    width, row_count = cen_hbm.shape
    cols = bat_hbm.shape[1]
    subset_count = eig_ref.shape[0]
    eig_part = subset_count // cls
    padded = upd.shape[0]
    first_row = r * row_count
    x_dev, y_dev, k_dev = (r + flip, c), (r, cy), (r, ck)
    near = [lax.rem(z + nz - d, nz) * NX + x for d in range(nz)]
    far = [row + flip for row in near]
    ahead = [lax.rem(z + d, nz) for d in range(nz)]

    def z_dev(d):
        return (ahead[d] * NX + x, c)

    barrier = pltpu.get_barrier_semaphore()
    partners = [x_dev, y_dev, k_dev] + [z_dev(d) for d in range(1, nz)]
    for dev in partners:
        pl.semaphore_signal(barrier, inc=1, device_id=dev, device_id_type=MESH)

    def part(col):
        return pl.ds(pl.multiple_of(col * width, width), width)

    eig_rows = pl.ds(pl.multiple_of(c * eig_part, eig_part), eig_part)
    own_eig = eig_hbm.at[eig_rows]
    local = [
        pltpu.make_async_copy(src, dst, local_sem.at[n])
        for n, (src, dst) in enumerate((
            (sub_hbm, sub_ref), (cen_hbm, cen.at[part(c)]), (bat_hbm, batch.at[r, part(c)]),
            (coef_hbm, coef_ref), (lab_hbm, lab_ref), (idx_hbm, idx_ref),
            (eig_hbm, eig_ref), (own_eig, eig.at[r, c]), (scale_hbm, scale_ref),
        ))
    ]
    for copy in local:
        copy.start()
    pl.semaphore_wait(barrier, len(partners))

    sent = []

    def send(src, dst, dev):
        n = len(sent)
        copy = pltpu.make_async_remote_copy(
            src_ref=src, dst_ref=dst, send_sem=send_sem.at[n], recv_sem=recv_sem.at[n],
            device_id=dev, device_id_type=MESH,
        )
        copy.start()
        sent.append(copy)

        def arrive(slot):
            pltpu.make_async_remote_copy(
                src_ref=slot, dst_ref=slot, send_sem=send_sem.at[n], recv_sem=recv_sem.at[n],
                device_id=dev, device_id_type=MESH,
            ).wait_recv()

        return arrive

    def slot(row, col):
        return batch.at[row, part(col)]

    def pass_on(row, col, dev):
        return send(slot(row, col), slot(row, col), dev)

    z_in = [None] + [send(bat_hbm, slot(r, c), z_dev(d)) for d in range(1, nz)]
    x_in = [send(bat_hbm, slot(r, c), x_dev)]
    y_in = [send(bat_hbm, slot(r, c), y_dev)]
    cen_y = send(cen_hbm, cen.at[part(c)], y_dev)
    near_in = [[send(bat_hbm, slot(r, c), k_dev)]]
    cen_k = send(cen_hbm, cen.at[part(c)], k_dev)

    for copy in local:
        copy.wait()
    coef = coef_ref[...]
    if padded > class_count:
        upd[...] = jnp.zeros_like(upd)
        upd[0:class_count, :] = coef
        coef = upd[...]
    coef_high, coef_low = split(coef)
    subset_local = sub_ref[...] - first_row
    pick_t = jnp.transpose(
        (
            lax.broadcasted_iota(jnp.int32, (row_count, subset_count), 0) == subset_local
        ).astype(jnp.float32)
    ).astype(jnp.bfloat16)
    for d in range(1, nz):
        z_in[d](slot(near[d], c))
        y_in.append(pass_on(near[d], c, y_dev))
        x_in.append(pass_on(near[d], c, x_dev))
        near_in.append([pass_on(near[d], c, k_dev)])
    cen_y(cen.at[part(cy)])
    cen_yk = send(cen.at[part(cy)], cen.at[part(cy)], k_dev)
    xy_in = []
    for d in range(nz):
        y_in[d](slot(near[d], cy))
        if d < nz - 1:
            xy_in.append(pass_on(near[d], cy, x_dev))
        near_in[d].append(pass_on(near[d], cy, k_dev))
    ez_in = [None] + [send(own_eig, eig.at[r, c], z_dev(d)) for d in range(1, nz)]
    far_in = [[] for _ in range(nz)]

    cen_k(cen.at[part(ck)])
    cen_yk(cen.at[part(cyk)])
    cen_wide = jnp.transpose(cen[...].astype(jnp.float32))
    cen_norm = jnp.sum(cen_wide * cen_wide, axis=1, keepdims=True)
    cen_rows = cen_wide.astype(jnp.bfloat16)

    later = []
    pick[...] = pick_t
    pick_own = pick[eig_rows, :]

    def part_pred(first, second):
        both = jnp.concatenate([batch[first], batch[second]], axis=1)
        wide = both.astype(jnp.float32)
        norm = jnp.sum(wide * wide, axis=0, keepdims=True)
        high, low = split(kernel_block(dot_nn(cen_rows, both), cen_norm, norm))
        later.append((first, second, high, low))
        return dot_nn(coef_high, high) + dot_nn(coef_high, low) + dot_nn(coef_low, high)

    def subset_part():
        for first, second, high, low in later:
            both = dot_nn(pick_own, high) + dot_nn(pick_own, low)
            for at, row in enumerate((first, second)):
                sk_own[row] = both[:, at * cols:(at + 1) * cols]
        later.clear()

    for i in range(nz - 1, -1, -1):
        x_in[i](slot(far[i], c))
        if i == nz - 1:
            xy_in.append(pass_on(far[i], c, y_dev))
        far_in[i].append(pass_on(far[i], c, k_dev))
    sum_in = []
    for d in range(0, nz, 2):
        for i in (d, d + 1):
            near_in[i][0](slot(near[i], ck))
            near_in[i][1](slot(near[i], cyk))
        both = part_pred(near[d], near[d + 1])
        for at, i in enumerate((d, d + 1)):
            pack(both[:, at * cols:(at + 1) * cols], xsend.at[i])
            sum_in.append(send(xsend.at[i], xrecv.at[i], x_dev))
        subset_part()
        for i in (d, d + 1):
            xy_in[i](slot(far[i], cy))
            far_in[i].append(pass_on(far[i], cy, k_dev))
    ey_in, ek_in = [], []

    def eig_on(row):
        ey_in.append((send(eig.at[row, c], eig.at[row, c], y_dev), row))
        ek_in.append((send(eig.at[row, c], eig.at[row, c], k_dev), row, ck))

    eig_on(r)
    ex_in = [send(own_eig, eig.at[r, c], x_dev)]
    for d in range(1, nz):
        ez_in[d](eig.at[near[d], c])
        ex_in.append(send(eig.at[near[d], c], eig.at[near[d], c], x_dev))
        eig_on(near[d])
    for d in range(0, nz, 2):
        for i in (d, d + 1):
            far_in[i][0](slot(far[i], ck))
            far_in[i][1](slot(far[i], cyk))
        both = part_pred(far[d], far[d + 1])
        for at, i in enumerate((d, d + 1)):
            acc[i] = both[:, at * cols:(at + 1) * cols]

    rs_in = [None] * nz
    for d in range(1, nz):
        sum_in[d](xrecv.at[d])
        pack(acc[d] + unpack(xrecv.at[d]), zsend.at[d - 1])
        rs_in[d] = send(zsend.at[d - 1], zrecv.at[d - 1], z_dev(nz - d))
    sum_in[0](xrecv.at[0])
    total = acc[0] + unpack(xrecv.at[0])
    subset_part()

    values = jnp.concatenate([sk_own[row] for row in range(rows)], axis=1)
    top = jnp.maximum(jnp.max(values, axis=1, keepdims=True), 1e-37)
    code = jnp.clip(jnp.ceil(jnp.log2(top) * STEPS) + 1.0, -32000.0, 32000.0)
    level = jnp.clip(jnp.round(values * (LARGEST * jnp.exp2(-code / STEPS))), -LARGEST, LARGEST)
    level = level.astype(jnp.int32).astype(jnp.int16)
    for row in range(rows):
        skq[r, c, row] = level[:, row * cols:(row + 1) * cols]
    codes = jnp.broadcast_to(code, (eig_part, cols))
    skq[r, c, rows] = codes.astype(jnp.int32).astype(jnp.int16)

    def kern_on(row, col, dev):
        return send(skq.at[row, col], skq.at[row, col], dev)

    kz_in = [None] + [kern_on(r, c, z_dev(d)) for d in range(1, nz)]
    kx_in = [kern_on(r, c, x_dev)]
    ky_in = [(kern_on(r, c, y_dev), r)]
    kk_in = [(kern_on(r, c, k_dev), r, ck)]

    for d in range(1, nz):
        rs_in[d](zrecv.at[d - 1])
        total += unpack(zrecv.at[d - 1])
    mine = far[0]
    pack(total, pred.at[mine])

    pz_in = [None] + [send(pred.at[mine], pred.at[mine], z_dev(d)) for d in range(1, nz)]
    px_in = [send(pred.at[mine], pred.at[mine], x_dev)]

    for d in range(1, nz):
        kz_in[d](skq.at[near[d], c])
        kx_in.append(kern_on(near[d], c, x_dev))
        ky_in.append((kern_on(near[d], c, y_dev), near[d]))
        kk_in.append((kern_on(near[d], c, k_dev), near[d], ck))
    for i in range(1, nz):
        pz_in[i](pred.at[far[i]])
        px_in.append(send(pred.at[far[i]], pred.at[far[i]], x_dev))
    for arrive, row in zip(ex_in, far):
        arrive(eig.at[row, c])
        eig_on(row)
    for arrive, row in zip(kx_in, far):
        arrive(skq.at[row, c])
        ky_in.append((kern_on(row, c, y_dev), row))
        kk_in.append((kern_on(row, c, k_dev), row, ck))
    for arrive, row in ey_in:
        arrive(eig.at[row, cy])
        ek_in.append((send(eig.at[row, cy], eig.at[row, cy], k_dev), row, cyk))
    for arrive, row in ky_in:
        arrive(skq.at[row, cy])
        kk_in.append((kern_on(row, cy, k_dev), row, cyk))
    for arrive, row, col in ek_in:
        arrive(eig.at[row, col])
    whole_high, whole_low = split(eig[...].reshape(rows * subset_count, eig_ref.shape[1]))
    own_high, own_low = split(eig_ref[...] * scale_ref[...])
    metric = dot_nt(own_high, whole_high) + dot_nt(own_high, whole_low)
    metric_high, metric_low = split(metric + dot_nt(own_low, whole_high))
    for arrive, row, col in kk_in:
        arrive(skq.at[row, col])
    flat = (rows * subset_count, cols)
    units = skq[:, :, rows].astype(jnp.int32).astype(jnp.float32).reshape(flat)
    units = jnp.exp2(units / STEPS) / LARGEST
    metric_both = jnp.concatenate([metric_high, metric_low], axis=0)
    for first in range(0, rows, 2):
        values = jnp.concatenate(
            [
                skq[:, :, row].astype(jnp.int32).astype(jnp.float32).reshape(flat) * units
                for row in (first, first + 1)
            ],
            axis=1,
        )
        high, low = split(values)
        two = dot_nn(metric_both, high)
        mixed = two[0:subset_count] + two[subset_count:] + dot_nn(metric_high, low)
        high, low = split(mixed)
        for at in range(2):
            lanes = slice(at * cols, (at + 1) * cols)
            sk[first + at, 0:subset_count, :] = high[:, lanes]
            sk[first + at, subset_count:2 * subset_count, :] = low[:, lanes]

    class_ids = lax.broadcasted_iota(jnp.int32, (padded, cols), 0) + c * class_count
    center_ids = lax.broadcasted_iota(jnp.int32, (row_count, cols), 0) + first_row

    leaving = []

    def use_pair(pair, error):
        grads, hits, kernels = [], [], []
        for row in pair:
            columns = pl.ds(pl.multiple_of(row * cols, cols), cols)
            n = 9 + len(leaving)
            leaving.append(
                pltpu.make_async_copy(pred_ref.at[row], pred_hbm.at[:, columns], local_sem.at[n])
            )
            value = unpack(pred.at[row])
            pred_ref[row] = value[0:class_count]
            leaving[-1].start()
            grads.append(value - (lab_ref[pl.ds(row, 1), :] == class_ids).astype(jnp.float32))
            kernels.append(sk[row])
        high, low = split(jnp.concatenate(grads, axis=1))
        kernel_pair = jnp.concatenate(kernels, axis=1)
        two = dot_nt(kernel_pair, high)
        error += two[0:subset_count] + two[subset_count:]
        return error + dot_nt(kernel_pair[0:subset_count], low), (pair, high, low)

    def scatter(update, moves):
        for pair, high, low in moves:
            hit = jnp.concatenate(
                [(idx_ref[pl.ds(row, 1), :] == center_ids).astype(jnp.float32) for row in pair],
                axis=1,
            ).astype(jnp.bfloat16)
            update += dot_nt(high, hit) + dot_nt(low, hit)
        return update

    error = jnp.zeros((subset_count, padded), jnp.float32)
    update = jnp.zeros((padded, row_count), jnp.float32)
    for d in range(0, nz, 2):
        error, move = use_pair((far[d], far[d + 1]), error)
        update = scatter(update, [move])
    moves = []
    for d in range(0, nz, 2):
        for i in (d, d + 1):
            px_in[i](pred.at[near[i]])
        error, move = use_pair((near[d], near[d + 1]), error)
        moves.append(move)

    upd[...] = coef - step_rate * scatter(update, moves)
    high, low = split(jnp.transpose(error))
    moved = dot_nn(high, pick_t) + dot_nn(low, pick_t)
    coef_ref[...] = (upd[...] + step_rate * moved)[0:class_count]
    leaving.append(pltpu.make_async_copy(coef_ref, new_hbm, local_sem.at[9 + rows]))
    leaving[-1].start()
    for copy in leaving:
        copy.wait()
    for copy in sent:
        copy.wait_send()


def fused_shards(
    rows, cls,
    centers, coefficients, batch_features, batch_labels, batch_index,
    subset_index, eigen_vectors, eigen_scale,
):
    row_count, width = centers.shape
    class_count = coefficients.shape[0]
    cols = batch_features.shape[0]
    subset_count, eig_count = eigen_vectors.shape
    padded = -(-class_count // 16) * 16
    nz = rows // NX
    copies = 16 * rows + 40
    f32, short = jnp.float32, jnp.int16
    hbm = pl.BlockSpec(memory_space=pltpu.HBM)
    return pl.pallas_call(
        functools.partial(fused_kernel, rows, cls, class_count),
        out_shape=(
            jax.ShapeDtypeStruct((class_count, rows * cols), f32),
            jax.ShapeDtypeStruct((class_count, row_count), f32),
        ),
        in_specs=[hbm] * 8,
        out_specs=(hbm, hbm),
        scratch_shapes=[
            pltpu.VMEM((rows, cls * width, cols), jnp.bfloat16),
            pltpu.VMEM((cls * width, row_count), jnp.bfloat16),
            pltpu.VMEM((rows, cls, subset_count // cls, eig_count), f32),
            pltpu.VMEM((rows, 2 * subset_count, cols), jnp.bfloat16),
            pltpu.VMEM((rows, subset_count // cls, cols), f32),
            pltpu.VMEM((rows, cls, rows + 1, subset_count // cls, cols), short),
            pltpu.VMEM((subset_count, row_count), jnp.bfloat16),
            pltpu.VMEM((nz, padded + 16, cols), short),
            pltpu.VMEM((nz, padded + 16, cols), short),
            pltpu.VMEM((nz, padded, cols), f32),
            pltpu.VMEM((nz - 1, padded + 16, cols), short),
            pltpu.VMEM((nz - 1, padded + 16, cols), short),
            pltpu.VMEM((rows, padded + 16, cols), short),
            pltpu.VMEM((padded, row_count), f32),
            pltpu.VMEM((rows, class_count, cols), f32),
            pltpu.VMEM((class_count, row_count), f32),
            pltpu.VMEM((rows, cols), jnp.int32),
            pltpu.VMEM((rows, cols), jnp.int32),
            pltpu.VMEM((1, subset_count), jnp.int32),
            pltpu.VMEM((subset_count, eig_count), f32),
            pltpu.VMEM((1, eig_count), f32),
            pltpu.SemaphoreType.DMA((copies,)),
            pltpu.SemaphoreType.DMA((copies,)),
            pltpu.SemaphoreType.DMA((rows + 10,)),
        ],
        compiler_params=pltpu.CompilerParams(
            collective_id=0, has_side_effects=True, vmem_limit_bytes=62 * 1024 * 1024
        ),
    )(
        centers.T, coefficients, batch_features.T,
        batch_labels.reshape(rows, cols), batch_index.reshape(rows, cols),
        subset_index.reshape(1, subset_count), eigen_vectors,
        eigen_scale.reshape(1, eig_count),
    )


def plain_shards(
    centers, coefficients, batch_features, batch_labels, batch_index,
    subset_index, eigen_vectors, eigen_scale,
):
    row_count = centers.shape[0]
    first_row = lax.axis_index("rows") * row_count
    subset_local = subset_index - first_row
    batch_rows = lax.all_gather(batch_features, "rows", axis=0, tiled=True)
    batch_whole = lax.all_gather(batch_rows, "cls", axis=1, tiled=True)
    batch_norm = square_norm(batch_whole)
    center_whole = lax.all_gather(centers, "cls", axis=1, tiled=True)
    inner = jnp.einsum("cd,bd->cb", center_whole, batch_whole, preferred_element_type=jnp.float32)
    kernel_centers = kernel_block(
        inner, square_norm(center_whole)[:, None], batch_norm[None, :]
    )
    subset_kernel = kernel_centers[subset_local]
    partial_pred = jnp.dot(coefficients, kernel_centers, precision=HIGHEST)
    class_count = coefficients.shape[0]
    class_start = lax.axis_index("cls") * class_count
    class_ids = jnp.arange(class_count, dtype=jnp.int32) + class_start
    targets = (batch_labels[None, :] == class_ids[:, None]).astype(jnp.float32)
    basis_part = jnp.dot(eigen_vectors.T, subset_kernel, precision=HIGHEST)
    predicted, basis_sum = lax.psum((partial_pred, basis_part), "rows")
    gradient = predicted - targets
    projected = jnp.dot(gradient, basis_sum.T, precision=HIGHEST)
    correction = jnp.dot(
        projected * eigen_scale[None, :], eigen_vectors.T, precision=HIGHEST
    )
    batch_local = batch_index - first_row
    is_owned = (batch_local >= 0) & (batch_local < row_count)
    batch_slot = jnp.where(is_owned, batch_local, row_count)
    updated = coefficients.at[:, batch_slot].add(-step_rate * gradient, mode="drop")
    updated = updated.at[:, subset_local].add(step_rate * correction)
    return (predicted, updated)


def solution(mesh):
    rows, cls = mesh.shape["rows"], mesh.shape["cls"]

    def shards(*args):
        cols = args[2].shape[0]
        fits = rows % (2 * NX) == 0 and cls == 2 * NCORE and cols % 128 == 0
        if fits:
            return fused_shards(rows, cls, *args)
        return plain_shards(*args)

    return jax.shard_map(
        shards,
        mesh=mesh,
        in_specs=(
            P("rows", "cls"), P("cls", "rows"), P("rows", "cls"), P(), P(),
            P("rows"), P("rows", None), P(),
        ),
        out_specs=(P("cls", None), P("cls", "rows")),
        check_vma=False,
    )
```

```python
import functools

import jax
import jax.numpy as jnp
from jax import lax
from jax.experimental import pallas as pl
from jax.experimental.pallas import tpu as pltpu
from jax.sharding import PartitionSpec as P

spread = 4.0
step_rate = 0.5
HIGHEST = lax.Precision.HIGHEST
MESH = pl.DeviceIdType.MESH
NX = 2
NCORE = 2
LARGEST = 32767.0
STEPS = 256.0


def kernel_block(inner, row_norm, col_norm):
    squared = row_norm + col_norm - 2.0 * inner
    return jnp.exp(-jnp.sqrt(jnp.maximum(squared, 0.0)) / spread)


def square_norm(features):
    return jnp.sum(jnp.square(features.astype(jnp.float32)), axis=1)


def dot_nt(a, b):
    return lax.dot_general(
        a, b, (((1,), (1,)), ((), ())), preferred_element_type=jnp.float32
    )


def dot_nn(a, b):
    return jnp.dot(a, b, preferred_element_type=jnp.float32)


def split(value):
    high = value.astype(jnp.bfloat16)
    low = (value - high.astype(jnp.float32)).astype(jnp.bfloat16)
    return high, low


def pack(value, slot):
    count = value.shape[0]
    top = jnp.maximum(jnp.max(jnp.abs(value), axis=0, keepdims=True), 1e-37)
    code = jnp.clip(jnp.ceil(jnp.log2(top) * STEPS) + 1.0, -32000.0, 32000.0)
    gain = LARGEST * jnp.exp2(-code / STEPS)
    level = jnp.clip(jnp.round(value * gain), -LARGEST, LARGEST)
    slot[0:count, :] = level.astype(jnp.int32).astype(jnp.int16)
    codes = jnp.broadcast_to(code, (16, value.shape[1]))
    slot[count:count + 16, :] = codes.astype(jnp.int32).astype(jnp.int16)


def unpack(slot):
    count = slot.shape[0] - 16
    codes = slot[count:count + 16, :].astype(jnp.int32).astype(jnp.float32)
    unit = jnp.exp2(codes[0:1, :] / STEPS) / LARGEST
    return slot[0:count, :].astype(jnp.int32).astype(jnp.float32) * unit


def fused_kernel(
    rows, cls, class_count,
    cen_hbm, coef_hbm, bat_hbm, lab_hbm, idx_hbm, sub_hbm, eig_hbm, scale_hbm,
    pred_hbm, new_hbm,
    batch, cen, eig, sk, sk_own, skq, pick, xsend, xrecv, acc, zsend, zrecv, pred, upd,
    pred_ref, coef_ref, lab_ref, idx_ref, sub_ref, eig_ref, scale_ref,
    send_sem, recv_sem, local_sem,
):
    nz = rows // NX
    r = lax.axis_index("rows")
    c = lax.axis_index("cls")
    z, x = r // NX, r % NX
    y, k = c // NCORE, c % NCORE
    flip = 1 - 2 * x
    cy = (1 - y) * NCORE + k
    ck = y * NCORE + (1 - k)
    cyk = (1 - y) * NCORE + (1 - k)
    width, row_count = cen_hbm.shape
    cols = bat_hbm.shape[1]
    subset_count = eig_ref.shape[0]
    eig_part = subset_count // cls
    padded = upd.shape[0]
    first_row = r * row_count
    x_dev, y_dev, k_dev = (r + flip, c), (r, cy), (r, ck)
    near = [lax.rem(z + nz - d, nz) * NX + x for d in range(nz)]
    far = [row + flip for row in near]
    ahead = [lax.rem(z + d, nz) for d in range(nz)]

    def z_dev(d):
        return (ahead[d] * NX + x, c)

    barrier = pltpu.get_barrier_semaphore()
    partners = [x_dev, y_dev, k_dev] + [z_dev(d) for d in range(1, nz)]
    for dev in partners:
        pl.semaphore_signal(barrier, inc=1, device_id=dev, device_id_type=MESH)

    def part(col):
        return pl.ds(pl.multiple_of(col * width, width), width)

    eig_rows = pl.ds(pl.multiple_of(c * eig_part, eig_part), eig_part)
    own_eig = eig_hbm.at[eig_rows]
    local = [
        pltpu.make_async_copy(src, dst, local_sem.at[n])
        for n, (src, dst) in enumerate((
            (sub_hbm, sub_ref), (cen_hbm, cen.at[part(c)]), (bat_hbm, batch.at[r, part(c)]),
            (coef_hbm, coef_ref), (lab_hbm, lab_ref), (idx_hbm, idx_ref),
            (eig_hbm, eig_ref), (own_eig, eig.at[r, c]), (scale_hbm, scale_ref),
        ))
    ]
    for copy in local:
        copy.start()
    pl.semaphore_wait(barrier, len(partners))

    sent = []

    def send(src, dst, dev):
        n = len(sent)
        copy = pltpu.make_async_remote_copy(
            src_ref=src, dst_ref=dst, send_sem=send_sem.at[n], recv_sem=recv_sem.at[n],
            device_id=dev, device_id_type=MESH,
        )
        copy.start()
        sent.append(copy)

        def arrive(slot):
            pltpu.make_async_remote_copy(
                src_ref=slot, dst_ref=slot, send_sem=send_sem.at[n], recv_sem=recv_sem.at[n],
                device_id=dev, device_id_type=MESH,
            ).wait_recv()

        return arrive

    def slot(row, col):
        return batch.at[row, part(col)]

    def pass_on(row, col, dev):
        return send(slot(row, col), slot(row, col), dev)

    z_in = [None] + [send(bat_hbm, slot(r, c), z_dev(d)) for d in range(1, nz)]
    x_in = [send(bat_hbm, slot(r, c), x_dev)]
    y_in = [send(bat_hbm, slot(r, c), y_dev)]
    cen_y = send(cen_hbm, cen.at[part(c)], y_dev)
    near_in = [[send(bat_hbm, slot(r, c), k_dev)]]
    cen_k = send(cen_hbm, cen.at[part(c)], k_dev)

    for copy in local:
        copy.wait()
    coef = coef_ref[...]
    if padded > class_count:
        upd[...] = jnp.zeros_like(upd)
        upd[0:class_count, :] = coef
        coef = upd[...]
    coef_high, coef_low = split(coef)
    subset_local = sub_ref[...] - first_row
    pick_t = jnp.transpose(
        (
            lax.broadcasted_iota(jnp.int32, (row_count, subset_count), 0) == subset_local
        ).astype(jnp.float32)
    ).astype(jnp.bfloat16)
    for d in range(1, nz):
        z_in[d](slot(near[d], c))
        y_in.append(pass_on(near[d], c, y_dev))
        x_in.append(pass_on(near[d], c, x_dev))
        near_in.append([pass_on(near[d], c, k_dev)])
    cen_y(cen.at[part(cy)])
    cen_yk = send(cen.at[part(cy)], cen.at[part(cy)], k_dev)
    xy_in = []
    for d in range(nz):
        y_in[d](slot(near[d], cy))
        if d < nz - 1:
            xy_in.append(pass_on(near[d], cy, x_dev))
        near_in[d].append(pass_on(near[d], cy, k_dev))
    ez_in = [None] + [send(own_eig, eig.at[r, c], z_dev(d)) for d in range(1, nz)]
    far_in = [[] for _ in range(nz)]

    cen_k(cen.at[part(ck)])
    cen_yk(cen.at[part(cyk)])
    cen_wide = jnp.transpose(cen[...].astype(jnp.float32))
    cen_norm = jnp.sum(cen_wide * cen_wide, axis=1, keepdims=True)
    cen_rows = cen_wide.astype(jnp.bfloat16)

    later = []
    pick[...] = pick_t
    pick_own = pick[eig_rows, :]

    def part_pred(first, second):
        both = jnp.concatenate([batch[first], batch[second]], axis=1)
        wide = both.astype(jnp.float32)
        norm = jnp.sum(wide * wide, axis=0, keepdims=True)
        high, low = split(kernel_block(dot_nn(cen_rows, both), cen_norm, norm))
        later.append((first, second, high, low))
        return dot_nn(coef_high, high) + dot_nn(coef_high, low) + dot_nn(coef_low, high)

    def subset_part():
        for first, second, high, low in later:
            both = dot_nn(pick_own, high) + dot_nn(pick_own, low)
            for at, row in enumerate((first, second)):
                sk_own[row] = both[:, at * cols:(at + 1) * cols]
        later.clear()

    for i in range(nz - 1, -1, -1):
        x_in[i](slot(far[i], c))
        if i == nz - 1:
            xy_in.append(pass_on(far[i], c, y_dev))
        far_in[i].append(pass_on(far[i], c, k_dev))
    sum_in = []
    for d in range(0, nz, 2):
        for i in (d, d + 1):
            near_in[i][0](slot(near[i], ck))
            near_in[i][1](slot(near[i], cyk))
        both = part_pred(near[d], near[d + 1])
        for at, i in enumerate((d, d + 1)):
            pack(both[:, at * cols:(at + 1) * cols], xsend.at[i])
            sum_in.append(send(xsend.at[i], xrecv.at[i], x_dev))
        subset_part()
        for i in (d, d + 1):
            xy_in[i](slot(far[i], cy))
            far_in[i].append(pass_on(far[i], cy, k_dev))
    ey_in, ek_in = [], []

    def eig_on(row):
        ey_in.append((send(eig.at[row, c], eig.at[row, c], y_dev), row))
        ek_in.append((send(eig.at[row, c], eig.at[row, c], k_dev), row, ck))

    eig_on(r)
    ex_in = [send(own_eig, eig.at[r, c], x_dev)]
    for d in range(1, nz):
        ez_in[d](eig.at[near[d], c])
        ex_in.append(send(eig.at[near[d], c], eig.at[near[d], c], x_dev))
        eig_on(near[d])
    for d in range(0, nz, 2):
        for i in (d, d + 1):
            far_in[i][0](slot(far[i], ck))
            far_in[i][1](slot(far[i], cyk))
        both = part_pred(far[d], far[d + 1])
        for at, i in enumerate((d, d + 1)):
            acc[i] = both[:, at * cols:(at + 1) * cols]

    rs_in = [None] * nz
    for d in range(1, nz):
        sum_in[d](xrecv.at[d])
        pack(acc[d] + unpack(xrecv.at[d]), zsend.at[d - 1])
        rs_in[d] = send(zsend.at[d - 1], zrecv.at[d - 1], z_dev(nz - d))
    sum_in[0](xrecv.at[0])
    total = acc[0] + unpack(xrecv.at[0])
    subset_part()

    values = jnp.concatenate([sk_own[row] for row in range(rows)], axis=1)
    top = jnp.maximum(jnp.max(values, axis=1, keepdims=True), 1e-37)
    code = jnp.clip(jnp.ceil(jnp.log2(top) * STEPS) + 1.0, -32000.0, 32000.0)
    level = jnp.clip(jnp.round(values * (LARGEST * jnp.exp2(-code / STEPS))), -LARGEST, LARGEST)
    level = level.astype(jnp.int32).astype(jnp.int16)
    for row in range(rows):
        skq[r, c, row] = level[:, row * cols:(row + 1) * cols]
    codes = jnp.broadcast_to(code, (eig_part, cols))
    skq[r, c, rows] = codes.astype(jnp.int32).astype(jnp.int16)

    def kern_on(row, col, dev):
        return send(skq.at[row, col], skq.at[row, col], dev)

    kz_in = [None] + [kern_on(r, c, z_dev(d)) for d in range(1, nz)]
    kx_in = [kern_on(r, c, x_dev)]
    ky_in = [(kern_on(r, c, y_dev), r)]
    kk_in = [(kern_on(r, c, k_dev), r, ck)]

    for d in range(1, nz):
        rs_in[d](zrecv.at[d - 1])
        total += unpack(zrecv.at[d - 1])
    mine = far[0]
    pack(total, pred.at[mine])

    pz_in = [None] + [send(pred.at[mine], pred.at[mine], z_dev(d)) for d in range(1, nz)]
    px_in = [send(pred.at[mine], pred.at[mine], x_dev)]

    for d in range(1, nz):
        kz_in[d](skq.at[near[d], c])
        kx_in.append(kern_on(near[d], c, x_dev))
        ky_in.append((kern_on(near[d], c, y_dev), near[d]))
        kk_in.append((kern_on(near[d], c, k_dev), near[d], ck))
    for arrive, row in zip(ex_in, far):
        arrive(eig.at[row, c])
        eig_on(row)
    for i in range(1, nz):
        pz_in[i](pred.at[far[i]])
        px_in.append(send(pred.at[far[i]], pred.at[far[i]], x_dev))
    for arrive, row in zip(kx_in, far):
        arrive(skq.at[row, c])
        ky_in.append((kern_on(row, c, y_dev), row))
        kk_in.append((kern_on(row, c, k_dev), row, ck))
    for arrive, row in ey_in:
        arrive(eig.at[row, cy])
        ek_in.append((send(eig.at[row, cy], eig.at[row, cy], k_dev), row, cyk))
    for arrive, row in ky_in:
        arrive(skq.at[row, cy])
        kk_in.append((kern_on(row, cy, k_dev), row, cyk))
    for arrive, row, col in ek_in:
        arrive(eig.at[row, col])
    whole_high, whole_low = split(eig[...].reshape(rows * subset_count, eig_ref.shape[1]))
    own_high, own_low = split(eig_ref[...] * scale_ref[...])
    metric = dot_nt(own_high, whole_high) + dot_nt(own_high, whole_low)
    metric_high, metric_low = split(metric + dot_nt(own_low, whole_high))
    for arrive, row, col in kk_in:
        arrive(skq.at[row, col])
    flat = (rows * subset_count, cols)
    units = skq[:, :, rows].astype(jnp.int32).astype(jnp.float32).reshape(flat)
    units = jnp.exp2(units / STEPS) / LARGEST
    metric_both = jnp.concatenate([metric_high, metric_low], axis=0)
    for first in range(0, rows, 2):
        values = jnp.concatenate(
            [
                skq[:, :, row].astype(jnp.int32).astype(jnp.float32).reshape(flat) * units
                for row in (first, first + 1)
            ],
            axis=1,
        )
        high, low = split(values)
        two = dot_nn(metric_both, high)
        mixed = two[0:subset_count] + two[subset_count:] + dot_nn(metric_high, low)
        high, low = split(mixed)
        for at in range(2):
            lanes = slice(at * cols, (at + 1) * cols)
            sk[first + at, 0:subset_count, :] = high[:, lanes]
            sk[first + at, subset_count:2 * subset_count, :] = low[:, lanes]

    class_ids = lax.broadcasted_iota(jnp.int32, (padded, cols), 0) + c * class_count
    center_ids = lax.broadcasted_iota(jnp.int32, (row_count, cols), 0) + first_row

    leaving = []

    def use_pair(pair, error):
        grads, hits, kernels = [], [], []
        for row in pair:
            columns = pl.ds(pl.multiple_of(row * cols, cols), cols)
            n = 9 + len(leaving)
            leaving.append(
                pltpu.make_async_copy(pred_ref.at[row], pred_hbm.at[:, columns], local_sem.at[n])
            )
            value = unpack(pred.at[row])
            pred_ref[row] = value[0:class_count]
            leaving[-1].start()
            grads.append(value - (lab_ref[pl.ds(row, 1), :] == class_ids).astype(jnp.float32))
            kernels.append(sk[row])
        high, low = split(jnp.concatenate(grads, axis=1))
        kernel_pair = jnp.concatenate(kernels, axis=1)
        two = dot_nt(kernel_pair, high)
        error += two[0:subset_count] + two[subset_count:]
        return error + dot_nt(kernel_pair[0:subset_count], low), (pair, high, low)

    def scatter(update, moves):
        for pair, high, low in moves:
            hit = jnp.concatenate(
                [(idx_ref[pl.ds(row, 1), :] == center_ids).astype(jnp.float32) for row in pair],
                axis=1,
            ).astype(jnp.bfloat16)
            update += dot_nt(high, hit) + dot_nt(low, hit)
        return update

    error = jnp.zeros((subset_count, padded), jnp.float32)
    update = jnp.zeros((padded, row_count), jnp.float32)
    for d in range(0, nz, 2):
        error, move = use_pair((far[d], far[d + 1]), error)
        update = scatter(update, [move])
    moves = []
    for d in range(0, nz, 2):
        for i in (d, d + 1):
            px_in[i](pred.at[near[i]])
        error, move = use_pair((near[d], near[d + 1]), error)
        moves.append(move)

    upd[...] = coef - step_rate * scatter(update, moves)
    high, low = split(jnp.transpose(error))
    moved = dot_nn(high, pick_t) + dot_nn(low, pick_t)
    coef_ref[...] = (upd[...] + step_rate * moved)[0:class_count]
    leaving.append(pltpu.make_async_copy(coef_ref, new_hbm, local_sem.at[9 + rows]))
    leaving[-1].start()
    for copy in leaving:
        copy.wait()
    for copy in sent:
        copy.wait_send()


def fused_shards(
    rows, cls,
    centers, coefficients, batch_features, batch_labels, batch_index,
    subset_index, eigen_vectors, eigen_scale,
):
    row_count, width = centers.shape
    class_count = coefficients.shape[0]
    cols = batch_features.shape[0]
    subset_count, eig_count = eigen_vectors.shape
    padded = -(-class_count // 16) * 16
    nz = rows // NX
    copies = 16 * rows + 40
    f32, short = jnp.float32, jnp.int16
    hbm = pl.BlockSpec(memory_space=pltpu.HBM)
    return pl.pallas_call(
        functools.partial(fused_kernel, rows, cls, class_count),
        out_shape=(
            jax.ShapeDtypeStruct((class_count, rows * cols), f32),
            jax.ShapeDtypeStruct((class_count, row_count), f32),
        ),
        in_specs=[hbm] * 8,
        out_specs=(hbm, hbm),
        scratch_shapes=[
            pltpu.VMEM((rows, cls * width, cols), jnp.bfloat16),
            pltpu.VMEM((cls * width, row_count), jnp.bfloat16),
            pltpu.VMEM((rows, cls, subset_count // cls, eig_count), f32),
            pltpu.VMEM((rows, 2 * subset_count, cols), jnp.bfloat16),
            pltpu.VMEM((rows, subset_count // cls, cols), f32),
            pltpu.VMEM((rows, cls, rows + 1, subset_count // cls, cols), short),
            pltpu.VMEM((subset_count, row_count), jnp.bfloat16),
            pltpu.VMEM((nz, padded + 16, cols), short),
            pltpu.VMEM((nz, padded + 16, cols), short),
            pltpu.VMEM((nz, padded, cols), f32),
            pltpu.VMEM((nz - 1, padded + 16, cols), short),
            pltpu.VMEM((nz - 1, padded + 16, cols), short),
            pltpu.VMEM((rows, padded + 16, cols), short),
            pltpu.VMEM((padded, row_count), f32),
            pltpu.VMEM((rows, class_count, cols), f32),
            pltpu.VMEM((class_count, row_count), f32),
            pltpu.VMEM((rows, cols), jnp.int32),
            pltpu.VMEM((rows, cols), jnp.int32),
            pltpu.VMEM((1, subset_count), jnp.int32),
            pltpu.VMEM((subset_count, eig_count), f32),
            pltpu.VMEM((1, eig_count), f32),
            pltpu.SemaphoreType.DMA((copies,)),
            pltpu.SemaphoreType.DMA((copies,)),
            pltpu.SemaphoreType.DMA((rows + 10,)),
        ],
        compiler_params=pltpu.CompilerParams(
            collective_id=0, has_side_effects=True, vmem_limit_bytes=62 * 1024 * 1024
        ),
    )(
        centers.T, coefficients, batch_features.T,
        batch_labels.reshape(rows, cols), batch_index.reshape(rows, cols),
        subset_index.reshape(1, subset_count), eigen_vectors,
        eigen_scale.reshape(1, eig_count),
    )


def plain_shards(
    centers, coefficients, batch_features, batch_labels, batch_index,
    subset_index, eigen_vectors, eigen_scale,
):
    row_count = centers.shape[0]
    first_row = lax.axis_index("rows") * row_count
    subset_local = subset_index - first_row
    batch_rows = lax.all_gather(batch_features, "rows", axis=0, tiled=True)
    batch_whole = lax.all_gather(batch_rows, "cls", axis=1, tiled=True)
    batch_norm = square_norm(batch_whole)
    center_whole = lax.all_gather(centers, "cls", axis=1, tiled=True)
    inner = jnp.einsum("cd,bd->cb", center_whole, batch_whole, preferred_element_type=jnp.float32)
    kernel_centers = kernel_block(
        inner, square_norm(center_whole)[:, None], batch_norm[None, :]
    )
    subset_kernel = kernel_centers[subset_local]
    partial_pred = jnp.dot(coefficients, kernel_centers, precision=HIGHEST)
    class_count = coefficients.shape[0]
    class_start = lax.axis_index("cls") * class_count
    class_ids = jnp.arange(class_count, dtype=jnp.int32) + class_start
    targets = (batch_labels[None, :] == class_ids[:, None]).astype(jnp.float32)
    basis_part = jnp.dot(eigen_vectors.T, subset_kernel, precision=HIGHEST)
    predicted, basis_sum = lax.psum((partial_pred, basis_part), "rows")
    gradient = predicted - targets
    projected = jnp.dot(gradient, basis_sum.T, precision=HIGHEST)
    correction = jnp.dot(
        projected * eigen_scale[None, :], eigen_vectors.T, precision=HIGHEST
    )
    batch_local = batch_index - first_row
    is_owned = (batch_local >= 0) & (batch_local < row_count)
    batch_slot = jnp.where(is_owned, batch_local, row_count)
    updated = coefficients.at[:, batch_slot].add(-step_rate * gradient, mode="drop")
    updated = updated.at[:, subset_local].add(step_rate * correction)
    return (predicted, updated)


def solution(mesh):
    rows, cls = mesh.shape["rows"], mesh.shape["cls"]

    def shards(*args):
        cols = args[2].shape[0]
        fits = rows % (2 * NX) == 0 and cls == 2 * NCORE and cols % 128 == 0
        if fits:
            return fused_shards(rows, cls, *args)
        return plain_shards(*args)

    return jax.shard_map(
        shards,
        mesh=mesh,
        in_specs=(
            P("rows", "cls"), P("cls", "rows"), P("rows", "cls"), P(), P(),
            P("rows"), P("rows", None), P(),
        ),
        out_specs=(P("cls", None), P("cls", "rows")),
        check_vma=False,
    )
```
